256 devices in a mesh: dp: 16 (over y, z_lo, core), tensor: 16 (over x, z_hi).
Axes of the slice: x: 4, y: 4, z: 8 (z_hi: 4, z_lo: 2; z = z_hi * 2 + z_lo), core: 2. Of those that a mesh axis runs over, the one named last changes fastest.
Arguments:
- ssm_input: bfloat16 [128, 64, 8192], P('dp', None, 'tensor'), may hold values from -6 to 6
- gate_input: bfloat16 [128, 64, 8192], P('dp', None, 'tensor'), may hold values from -6 to 6
- write_basis: bfloat16 [128, 64, 4, 128], P('dp'), may hold values from -4 to 4
- read_basis: bfloat16 [128, 64, 4, 128], P('dp'), may hold values from -4 to 4
- step_raw: float32 [128, 128, 64], P('dp', 'tensor'), may hold values from -4 to 4
- step_bias: float32 [128], P('tensor'), may hold values from -1 to 1
- decay_rate: float32 [128], P('tensor'), may hold values from 0.003 to 0.12
- skip_gain: float32 [128], P('tensor'), may hold values from 0.5 to 1.5
- norm_gain: float32 [8192], P('tensor'), may hold values from 0.1 to 1.9
- out_weight: bfloat16 [8192, 8192], P('tensor'), may hold values from -0.09375 to 0.09375
- ssm_states: bfloat16 [128, 128, 64, 128], P('dp', 'tensor'), may hold values from -6 to 6
- anchor: int32 [128], replicated, may hold values from 0 to 127, as said below
- tool_length: int32 [128], P('dp'), may hold values from 1 to 64, 4096 in all
Outputs:
- layer_out: bfloat16 [128, 64, 8192], P('dp', None, 'tensor')
- new_states: bfloat16 [128, 128, 64, 128], P('dp', 'tensor')
The draws below stay inside these ranges and needn't reach their ends.
Inputs may be any that keep to these rules, and one draw needn't show every extreme that they name: anchor is a permutation of 0 .. 127; row i lies in group i // 8 and takes over row anchor[i] of group anchor[i] // 8. From one group to another different group at most 2 rows move, and at most 4 rows leave one group; both bounds are reached in every draw.
All inputs are finite; a program needn't handle non-finite values. No bound on the sum of `tool_length` on one device may be relied on, other than what follows from the above.
Results may differ from the reference program's by a relative error of at most 0.0049.
Values may be sent and summed in bfloat16 or wider, within the bound.
No kernel may reach another device: no remote copies, remote signals or barrier semaphores. Data moves between devices by JAX's collectives and lax.ppermute only.
A program may use at most 128 MiB of HBM per device.

```python
import math
import jax
import jax.numpy as jnp
import numpy as np
from jax import lax

D = 8192
HEADS = 128
HEAD_DIM = 64
STATE = 128
NGROUPS = 4
ROWS = 8
NEW = 64
GROUPS = 16
ALL_ROWS = 128


def draw_anchor(key, part):
    key = jax.random.fold_in(key, 7)
    key_shift, key_source, key_target = jax.random.split(key, 3)
    first = jnp.int32(1)
    second = jax.random.randint(key_shift, (), 2, GROUPS).astype(jnp.int32)
    slot_cap = ROWS // 4

    def shuffle(subkey):
        return jax.random.permutation(subkey, ROWS).astype(jnp.int32)
    source_perm = jax.vmap(shuffle)(jax.random.split(key_source, GROUPS))
    target_perm = jax.vmap(shuffle)(jax.random.split(key_target, GROUPS))
    group_ids = jnp.arange(GROUPS, dtype=jnp.int32)
    from_first = (group_ids - first) % GROUPS
    from_second = (group_ids - second) % GROUPS
    items = jnp.concatenate([from_first[:, None] * ROWS + source_perm[from_first, :slot_cap], from_second[:, None] * ROWS + source_perm[from_second, slot_cap:2 * slot_cap], group_ids[:, None] * ROWS + source_perm[:, 2 * slot_cap:]], axis=1)
    placed = jnp.zeros((GROUPS, ROWS), jnp.int32).at[group_ids[:, None], target_perm].set(items)
    return placed.reshape(GROUPS * ROWS)


def strengthened(drawn, rng, source, target, blocks, factor):
    owner, partner = [(jnp.arange(drawn.shape[dim]) // (drawn.shape[dim] // blocks)).reshape([-1 if axis == dim else 1 for axis in range(drawn.ndim)]) for dim in (source, target)]
    chosen = jax.random.permutation(rng, blocks)[partner]
    strong = (owner == chosen) | (owner == (partner + blocks // 2) % blocks)
    return jnp.where(strong, factor * drawn, drawn)


def levels(key, shape, shards, least, high):
    loudness, own = 1.0, jax.random.fold_in(key, 6)
    for position, parts in shards:
        steps = jnp.exp(jax.random.uniform(jax.random.fold_in(own, position), (parts,), jnp.float32, least / len(shards), high / len(shards)))
        loudness = loudness * jnp.repeat(steps, shape[position] // parts).reshape([-1 if axis == position else 1 for axis in range(len(shape))])
    return loudness


def length_profile(amount, total, reach, skew):
    loads = [(1 << 20) // math.isqrt(rank ** skew) + 1 for rank in range(2, amount + 1)]
    surplus, holding = total - reach - (amount - 1), [1] * (amount - 1)
    while surplus > 0:
        movable = [i for i in range(amount - 1) if holding[i] < reach]
        mass, budget = sum([loads[i] for i in movable]), surplus
        for i in movable:
            extra = min(reach - holding[i], max(1, budget * loads[i] // mass), surplus)
            holding[i] = holding[i] + extra
            surplus = surplus - extra
    return np.array([reach] + holding)


def uneven(rng, number_of, total, bound, lean):
    if number_of == 2:
        one = jax.random.randint(rng, (), max(1, total - bound), min(bound, total - 1) + 1)
        return jnp.stack([one, total - one])
    sizes = jnp.asarray(length_profile(number_of, total, bound, lean), jnp.int32)
    pairs = (number_of - 1) // 2
    donor, sink = sizes[1:1 + 2 * pairs:2], sizes[2:2 + 2 * pairs:2]
    slack = jnp.minimum(donor - 1, bound - sink)
    moved = jax.random.randint(jax.random.fold_in(rng, 1), (pairs,), 0, 1 << 20) % (slack + 1)
    sizes = sizes.at[1:1 + 2 * pairs:2].set(donor - moved).at[2:2 + 2 * pairs:2].set(sink + moved)
    return sizes[jax.random.permutation(jax.random.fold_in(rng, 2), number_of)]


def scatter_about(rng, dims, spread, reach, cuts=(), kind=jnp.bfloat16):
    result = jax.random.normal(rng, dims, jnp.float32) * spread
    if len(cuts) > 0:
        result = levels(rng, dims, cuts, -0.22, 0.18) * result
    return jnp.clip(result, min=-reach, max=reach).astype(kind)


def noise_with(rng, dims, width, most, shards, heavy, held_as=jnp.bfloat16):
    values = width * jax.random.normal(rng, dims, jnp.float32)
    if shards:
        values = values * levels(rng, dims, shards, -0.22, 0.18)
    return jnp.clip(strengthened(values, jax.random.fold_in(rng, 3), *heavy), -most, most).astype(held_as)


def setup_inputs(seed: int = 0) -> dict:
    arg_keys = jax.random.split(jax.random.key(seed), 14)
    return {
        "ssm_input": scatter_about(arg_keys[0], (ALL_ROWS, NEW, HEADS * HEAD_DIM), 1.0, 6.0, ((0, 16), (2, 16))),
        "gate_input": scatter_about(arg_keys[1], (ALL_ROWS, NEW, HEADS * HEAD_DIM), 1.0, 6.0, ((0, 16), (2, 16))),
        "write_basis": scatter_about(arg_keys[2], (ALL_ROWS, NEW, NGROUPS, STATE), 0.3, 4.0, ((0, 16),)),
        "read_basis": scatter_about(arg_keys[3], (ALL_ROWS, NEW, NGROUPS, STATE), 0.3, 4.0, ((0, 16),)),
        "step_raw": scatter_about(arg_keys[4], (ALL_ROWS, HEADS, NEW), 1.0, 4.0, ((0, 16), (1, 16)), jnp.float32),
        "step_bias": jnp.clip(jax.random.uniform(arg_keys[5], (HEADS,), jnp.float32, -1.0, 1.0) * levels(arg_keys[5], (HEADS,), ((0, 16),), -0.4, 0.0), -1.0, 1.0),
        "decay_rate": jnp.clip(jnp.exp(math.log(0.12) - 3.6888794 * jax.random.uniform(arg_keys[6], (HEADS,), jnp.float32) ** levels(arg_keys[6], (HEADS,), ((0, 16),), -0.2, 0.2)), 0.003, 0.12),
        "skip_gain": jnp.clip(0.5 + 1.0 * jax.random.uniform(arg_keys[7], (HEADS,), jnp.float32) ** levels(arg_keys[7], (HEADS,), ((0, 16),), -0.2, 0.2), 0.5, 1.5),
        "norm_gain": jnp.clip(1.0 + 0.18 * jax.random.normal(arg_keys[8], (HEADS * HEAD_DIM,), jnp.float32), 0.1, 1.9),
        "out_weight": noise_with(arg_keys[9], (HEADS * HEAD_DIM, D), (HEADS * HEAD_DIM) ** -0.5, 0.09375, ((0, 16),), (0, 1, 16, 2.0)),
        "ssm_states": scatter_about(arg_keys[10], (ALL_ROWS, HEADS, HEAD_DIM, STATE), 1.0, 6.0, ((0, 16), (1, 16))),
        "anchor": draw_anchor(jax.random.fold_in(arg_keys[13], 71), 0),
        "tool_length": uneven(arg_keys[12], ALL_ROWS, ALL_ROWS * NEW // 2, NEW, 2).astype(jnp.int32),
    }


def reference(ssm_input, gate_input, write_basis, read_basis, step_raw, step_bias, decay_rate, skip_gain, norm_gain, out_weight, ssm_states, anchor, tool_length):
    row_total = ssm_input.shape[0]
    group_heads = HEADS // NGROUPS
    start_state = ssm_states[anchor].astype(jnp.float32).reshape(row_total, NGROUPS, group_heads, HEAD_DIM, STATE)
    positions = jnp.arange(NEW, dtype=jnp.int32)
    live_mask = (positions[None, :] < tool_length[:, None]).astype(jnp.float32)
    step_size = jax.nn.softplus(step_raw + step_bias[None, :, None]) * live_mask[:, None, :]
    decay = jnp.exp(-decay_rate[None, :, None] * step_size)
    input_heads = ssm_input.astype(jnp.float32).reshape(row_total, NEW, NGROUPS, group_heads, HEAD_DIM)
    write_all = write_basis.astype(jnp.float32)
    read_all = read_basis.astype(jnp.float32)

    def advance(state_now, step_inputs):
        decay_now, size_now, input_now, write_now, read_now = step_inputs
        decay_part = decay_now.reshape(row_total, NGROUPS, group_heads)[:, :, :, None, None]
        scaled = size_now.reshape(row_total, NGROUPS, group_heads)[:, :, :, None] * input_now
        state_now = decay_part * state_now + scaled[..., None] * write_now[:, :, None, None, :]
        output_now = jnp.einsum('agdpn,agn->agdp', state_now, read_now, precision=lax.Precision.HIGHEST)
        return (state_now, output_now)
    step_inputs = (jnp.moveaxis(decay, 2, 0), jnp.moveaxis(step_size, 2, 0), jnp.moveaxis(input_heads, 1, 0), jnp.moveaxis(write_all, 1, 0), jnp.moveaxis(read_all, 1, 0))
    final_state, outputs = lax.scan(advance, start_state, step_inputs)
    outputs = jnp.moveaxis(outputs, 0, 1)
    skip_part = skip_gain.reshape(NGROUPS, group_heads)[None, None, :, :, None] * input_heads
    outputs = (outputs + skip_part) * live_mask[:, :, None, None, None]
    gate_heads = gate_input.astype(jnp.float32).reshape(row_total, NEW, NGROUPS, group_heads, HEAD_DIM)
    gated = outputs * jax.nn.silu(gate_heads)
    mean_square = lax.optimization_barrier(jnp.mean(gated * gated, axis=(3, 4), keepdims=True))
    normed = (gated * lax.rsqrt(mean_square + 1e-05) * norm_gain.reshape(NGROUPS, group_heads, HEAD_DIM)).astype(jnp.bfloat16)
    flat_normed = normed.reshape(row_total * NEW, HEADS * HEAD_DIM)
    layer_out = jnp.dot(flat_normed, out_weight, preferred_element_type=jnp.float32).astype(jnp.bfloat16)
    layer_out = layer_out.reshape(row_total, NEW, D)
    new_states = final_state.reshape(row_total, HEADS, HEAD_DIM, STATE).astype(jnp.bfloat16)
    return (layer_out, new_states)
```

```python
import functools
import jax
import jax.numpy as jnp
import numpy as np
from jax import lax
from jax.experimental import pallas as pl
from jax.experimental.pallas import tpu as pltpu
from jax.sharding import Mesh, PartitionSpec as P

F32 = jnp.float32
BF16 = jnp.bfloat16
HIGH = lax.Precision.HIGHEST
SIZES = {"y": 4, "zl": 2, "c": 2, "x": 4, "zh": 4}
ROWS = 8
HALF = 4
NEW = 64
NT = (((1,), (1,)), ((), ()))
TN = (((0,), (0,)), ((), ()))


def shift(value, axis, step):
    size = SIZES[axis]
    return lax.ppermute(value, axis, [(i, (i + step) % size) for i in range(size)])


def ssm_kernel(source_count, has_alias, sc, x_ref, g_ref, b_ref, c_ref, dt_ref, par_ref, *refs):
    sources = refs[:source_count]
    refs = refs[source_count + int(has_alias) :]
    gated_ref, sq_ref, new_ref, held = refs
    r = pl.program_id(0)
    length = sc[HALF + r]
    code = sc[2 * HALF + r]
    for which, source in enumerate(sources):

        @pl.when(code == which)
        def _():
            held[...] = source[0]

    lane = lax.broadcasted_iota(jnp.int32, (NEW, 128), 1)
    sub = lax.broadcasted_iota(jnp.int32, (NEW, 128), 0)
    within = lane & 63
    causal = within <= sub
    eye = within == sub
    first_half = lane < 64
    live = sub < length
    rows = lax.broadcasted_iota(jnp.int32, (128, 128), 0)
    cols = lax.broadcasted_iota(jnp.int32, (128, 128), 1)
    same = (rows >> 6) == (cols >> 6)
    same_head = jnp.where(same, 1.0, 0.0).astype(F32)
    upper = jnp.where(same & (rows <= cols), 1.0, 0.0).astype(F32)
    bias4, rate4, skip4 = par_ref[0], par_ref[1], par_ref[2]
    raw = dt_ref[0] + bias4
    soft = jnp.maximum(raw, 0.0) + jnp.log1p(jnp.exp(-jnp.abs(raw)))
    lane4 = lax.broadcasted_iota(jnp.int32, (4, 128), 1) & 63
    dt4 = jnp.where(lane4 < length, soft, 0.0)
    a4 = -rate4 * dt4
    pieces = [jnp.where(causal, a4[p : p + 1], 0.0) for p in range(4)]
    pieces += [jnp.where(eye, dt4[p : p + 1], 0.0) for p in range(4)]
    spread = jnp.dot(
        jnp.concatenate(pieces, axis=0), same_head, precision=HIGH, preferred_element_type=F32
    )
    ds4 = jnp.dot(a4, upper, precision=HIGH, preferred_element_type=F32)
    tot4 = jnp.dot(a4, same_head, precision=HIGH, preferred_element_type=F32)
    c_val = c_ref[0]
    b_val = b_ref[0]
    bb = jnp.concatenate([b_val, b_val], axis=0)
    affinity = lax.dot_general(c_val, bb, NT, preferred_element_type=F32)
    affinity = jnp.where(causal, affinity, 0.0)
    squares = jnp.zeros((NEW, 128), F32)
    for p in range(4):
        ds_t = spread[p * NEW : (p + 1) * NEW]
        dt_t = spread[(4 + p) * NEW : (5 + p) * NEW]
        mix = affinity * jnp.exp(ds_t - ds4[p : p + 1]) * dt4[p : p + 1]
        hi = mix.astype(BF16)
        lo = (mix - hi.astype(F32)).astype(BF16)
        xf = x_ref[0, :, p * 128 : (p + 1) * 128].astype(F32)
        blocks = jnp.concatenate(
            [jnp.where(first_half, xf, 0.0), jnp.where(first_half, 0.0, xf)], axis=0
        ).astype(BF16)
        inner = jnp.dot(hi, blocks, preferred_element_type=F32) + jnp.dot(
            lo, blocks, preferred_element_type=F32
        )
        state = held[2 * p : 2 * p + 2].reshape(128, 128)
        carried = lax.dot_general(c_val, state, NT, preferred_element_type=F32)
        out = inner + carried * jnp.exp(ds_t) + skip4[p : p + 1] * xf
        gf = g_ref[0, :, p * 128 : (p + 1) * 128].astype(F32)
        gated = jnp.where(live, out * (gf / (1.0 + jnp.exp(-gf))), 0.0)
        gated_ref[0, :, p * 128 : (p + 1) * 128] = gated
        squares = squares + gated * gated
        weighted = xf * (jnp.exp(tot4[p : p + 1] - ds_t) * dt_t)
        w_hi = weighted.astype(BF16)
        w_lo = (weighted - w_hi.astype(F32)).astype(BF16)
        both = jnp.concatenate([w_hi, w_lo], axis=0)
        update = lax.dot_general(both, bb, TN, preferred_element_type=F32)
        e_tot = jnp.exp(tot4[p : p + 1])
        for k in range(2):
            kept = state[k * 64 : (k + 1) * 64].astype(F32) * e_tot[:, k * 64 : k * 64 + 1]
            new_ref[0, 2 * p + k] = (kept + update[k * 64 : (k + 1) * 64]).astype(BF16)
    ones = jnp.ones((8, 128), F32)
    sq = lax.dot_general(ones, squares, NT, precision=HIGH, preferred_element_type=F32)
    sq_ref[0] = sq[0:1]


def run_ssm(table, x, gate, b, c, dt, par, sources, alias):
    count = len(sources)
    row3 = lambda r, sc: (sc[r], 0, 0)
    in_specs = [
        pl.BlockSpec((1, NEW, 512), row3),
        pl.BlockSpec((1, NEW, 512), row3),
        pl.BlockSpec((1, NEW, 128), row3),
        pl.BlockSpec((1, NEW, 128), row3),
        pl.BlockSpec((1, 4, 128), row3),
        pl.BlockSpec((3, 4, 128), lambda r, sc: (0, 0, 0)),
    ]
    for k in range(count):
        in_specs.append(
            pl.BlockSpec(
                (1, 8, 64, 128), lambda r, sc, k=k: (sc[(3 + k) * HALF + r], 0, 0, 0)
            )
        )
    operands = [table, x, gate, b, c, dt, par, *sources]
    aliases = {}
    if alias is not None:
        in_specs.append(pl.BlockSpec(memory_space=pl.ANY))
        aliases = {len(operands): 2}
        operands.append(alias)
    return pl.pallas_call(
        functools.partial(ssm_kernel, count, alias is not None),
        grid_spec=pltpu.PrefetchScalarGridSpec(
            num_scalar_prefetch=1,
            grid=(HALF,),
            in_specs=in_specs,
            out_specs=[
                pl.BlockSpec((1, NEW, 512), lambda r, sc: (r, 0, 0)),
                pl.BlockSpec((1, 1, NEW), lambda r, sc: (r, 0, 0)),
                pl.BlockSpec((1, 8, 64, 128), lambda r, sc: (sc[r], 0, 0, 0)),
            ],
            scratch_shapes=[pltpu.VMEM((8, 64, 128), BF16)],
        ),
        out_shape=[
            jax.ShapeDtypeStruct((HALF, NEW, 512), F32),
            jax.ShapeDtypeStruct((HALF, 1, NEW), F32),
            jax.ShapeDtypeStruct((ROWS, 8, 64, 128), BF16),
        ],
        input_output_aliases=aliases,
        compiler_params=pltpu.CompilerParams(vmem_limit_bytes=32 << 20),
        cost_estimate=pl.CostEstimate(flops=300_000_000, bytes_accessed=4 << 20, transcendentals=0),
        name="ssm",
    )(*operands)


def normalise(gated, sums, gain, held):
    rows = lax.broadcasted_iota(jnp.int32, (NEW, NEW), 0)
    cols = lax.broadcasted_iota(jnp.int32, (NEW, NEW), 1)
    for r in range(HALF):
        total = sums[0][r] + sums[1][r] + sums[2][r] + sums[3][r]
        scale = lax.rsqrt(total / 2048.0 + 1e-05)
        column = jnp.sum(jnp.where(rows == cols, scale, 0.0), axis=1, keepdims=True)
        held[r * NEW : (r + 1) * NEW] = (gated[r] * column * gain[...]).astype(BF16)


def project_kernel(sc, gated, s0, s1, s2, s3, gain, w, out, held):
    @pl.when(pl.program_id(0) == 0)
    def _():
        normalise(gated, (s0, s1, s2, s3), gain, held)

    out[...] = jnp.dot(held[...], w[...], preferred_element_type=F32).astype(BF16)


def norm_specs():
    return [
        pl.BlockSpec((HALF, NEW, 512), lambda j, sc: (0, 0, 0)),
        *[pl.BlockSpec((HALF, 1, NEW), lambda j, sc: (0, 0, 0)) for _ in range(4)],
        pl.BlockSpec((1, 512), lambda j, sc: (0, 0)),
    ]


def project(place, step, gated, sums, gain, w):
    rows = HALF * NEW
    return pl.pallas_call(
        project_kernel,
        grid_spec=pltpu.PrefetchScalarGridSpec(
            num_scalar_prefetch=1,
            grid=(2,),
            in_specs=[
                *norm_specs(),
                pl.BlockSpec((512, 1024), lambda j, sc: (0, ((sc[0] + step) % 4) * 2 + j)),
            ],
            out_specs=pl.BlockSpec((rows, 1024), lambda j, sc: (0, j)),
            scratch_shapes=[pltpu.VMEM((rows, 512), BF16)],
        ),
        out_shape=jax.ShapeDtypeStruct((rows, 2048), BF16),
        compiler_params=pltpu.CompilerParams(vmem_limit_bytes=32 << 20),
        cost_estimate=pl.CostEstimate(
            flops=2 * rows * 512 * 2048, bytes_accessed=4 << 20, transcendentals=0
        ),
        name="project",
    )(place, gated, *sums, gain, w)


def own_kernel(sc, gated, s0, s1, s2, s3, gain, w, r1, r2, r3, z0, z1, z2, z3, held):
    j = pl.program_id(0)

    @pl.when(j == 0)
    def _():
        normalise(gated, (s0, s1, s2, s3), gain, held)

    value = jnp.dot(held[...], w[...], preferred_element_type=F32)
    value = value + r1[...].astype(F32) + r2[...].astype(F32) + r3[...].astype(F32)

    @pl.when(j == 0)
    def _():
        z0[...] = value

    for k, ref in ((1, z1), (2, z2), (3, z3)):

        @pl.when(j == k)
        def _():
            ref[...] = value.astype(BF16)


def own_project(place, gated, sums, gain, w, received):
    rows = HALF * NEW
    whole = pl.BlockSpec((rows, 512), lambda j, sc: (0, 0))
    return pl.pallas_call(
        own_kernel,
        grid_spec=pltpu.PrefetchScalarGridSpec(
            num_scalar_prefetch=1,
            grid=(4,),
            in_specs=[
                *norm_specs(),
                pl.BlockSpec((512, 512), lambda j, sc: (0, sc[0] * 4 + (sc[1] + j) % 4)),
                *[
                    pl.BlockSpec((rows, 512), lambda j, sc: (0, (sc[1] + j) % 4))
                    for _ in range(3)
                ],
            ],
            out_specs=[whole] * 4,
            scratch_shapes=[pltpu.VMEM((rows, 512), BF16)],
        ),
        out_shape=[
            jax.ShapeDtypeStruct((rows, 512), F32),
            *[jax.ShapeDtypeStruct((rows, 512), BF16) for _ in range(3)],
        ],
        compiler_params=pltpu.CompilerParams(vmem_limit_bytes=32 << 20),
        cost_estimate=pl.CostEstimate(
            flops=2 * rows * 512 * 2048, bytes_accessed=7 << 20, transcendentals=0
        ),
        name="own_project",
    )(place, gated, *sums, gain, w, *received)


def finish_kernel(sc, z0, r1, r2, r3, *refs):
    out = refs[-1]
    value = z0[...] + r1[...].astype(F32) + r2[...].astype(F32) + r3[...].astype(F32)
    out[0] = value.astype(BF16)


def finish(table, parts, alias):
    block = pl.BlockSpec((NEW, 512), lambda r, sc: (r, 0))
    in_specs = [block] * 4
    operands = [table, *parts]
    aliases = {}
    if alias is not None:
        in_specs.append(pl.BlockSpec(memory_space=pl.ANY))
        aliases = {len(operands): 0}
        operands.append(alias)
    return pl.pallas_call(
        finish_kernel,
        grid_spec=pltpu.PrefetchScalarGridSpec(
            num_scalar_prefetch=1,
            grid=(HALF,),
            in_specs=in_specs,
            out_specs=pl.BlockSpec((1, NEW, 512), lambda r, sc: (sc[r], 0, 0)),
        ),
        out_shape=jax.ShapeDtypeStruct((ROWS, NEW, 512), BF16),
        input_output_aliases=aliases,
        cost_estimate=pl.CostEstimate(flops=1_000_000, bytes_accessed=2 << 20, transcendentals=0),
        name="finish",
    )(*operands)


def pick_kernel(count, sc, *refs):
    sources, outs = refs[: count * 3], refs[count * 3 :]
    q = pl.program_id(0)
    for k in range(3):
        code = sc[k * HALF + q]
        for which in range(count):

            @pl.when(code == which)
            def _():
                outs[k][...] = sources[k * count + which][...]


def pick(table, sources):
    count = len(sources)
    block = (1, 8, 64, 128)
    in_specs = [
        pl.BlockSpec(block, lambda q, sc, k=k: (sc[3 * HALF + k * HALF + q], 0, 0, 0))
        for k in range(3)
        for _ in range(count)
    ]
    return pl.pallas_call(
        functools.partial(pick_kernel, count),
        grid_spec=pltpu.PrefetchScalarGridSpec(
            num_scalar_prefetch=1,
            grid=(HALF,),
            in_specs=in_specs,
            out_specs=[pl.BlockSpec(block, lambda q, sc: (q, 0, 0, 0))] * 3,
        ),
        out_shape=[jax.ShapeDtypeStruct((HALF, 8, 64, 128), BF16)] * 3,
        compiler_params=pltpu.CompilerParams(vmem_limit_bytes=32 << 20),
        cost_estimate=pl.CostEstimate(flops=1, bytes_accessed=8 << 20, transcendentals=0),
        name="pick",
    )(table, *(list(sources) * 3))


def copy_kernel(sc, source, out):
    out[...] = source[...]


def take_rows(table, states):
    block = (1, 8, 64, 128)
    return pl.pallas_call(
        copy_kernel,
        grid_spec=pltpu.PrefetchScalarGridSpec(
            num_scalar_prefetch=1,
            grid=(HALF,),
            in_specs=[pl.BlockSpec(block, lambda q, sc: (sc[q], 0, 0, 0))],
            out_specs=pl.BlockSpec(block, lambda q, sc: (q, 0, 0, 0)),
        ),
        out_shape=jax.ShapeDtypeStruct((HALF, 8, 64, 128), BF16),
        cost_estimate=pl.CostEstimate(flops=1, bytes_accessed=1 << 20, transcendentals=0),
        name="take_rows",
    )(table, states)


def chosen(mask, values):
    return jnp.sum(jnp.where(mask, values, 0), axis=-1, dtype=jnp.int32)


def local(
    ssm_input,
    gate_input,
    write_basis,
    read_basis,
    step_raw,
    step_bias,
    decay_rate,
    skip_gain,
    norm_gain,
    out_weight,
    ssm_states,
    anchor,
    tool_length,
):
    y, zl, c = lax.axis_index("y"), lax.axis_index("zl"), lax.axis_index("c")
    x, zh = lax.axis_index("x"), lax.axis_index("zh")
    me = (y * 2 + zl) * 2 + c
    ids = jnp.arange(ROWS * 16, dtype=jnp.int32)
    dest = ids // ROWS
    source, source_row = anchor // ROWS, anchor % ROWS
    moving = source != dest
    earlier = ids[None, :] < ids[:, None]

    same_source = moving[None, :] & (source[None, :] == source[:, None]) & earlier
    leave_slot = jnp.sum(same_source, axis=1, dtype=jnp.int32)
    slots = jnp.arange(HALF, dtype=jnp.int32)
    leaving = (moving & (source == me))[None, :] & (leave_slot[None, :] == slots[:, None])
    buf = take_rows(chosen(leaving, source_row[None, :]), ssm_states)
    across = shift(buf, "zl", 1)
    beside = shift(buf, "c", 1)

    lo = me * ROWS
    mine_source = lax.dynamic_slice_in_dim(source, lo, ROWS)
    mine_row = lax.dynamic_slice_in_dim(source_row, lo, ROWS)
    mine_moving = mine_source != me
    local_ids = jnp.arange(ROWS, dtype=jnp.int32)
    before = (mine_moving[None, :] == mine_moving[:, None]) & (
        local_ids[None, :] < local_ids[:, None]
    )
    rank = jnp.sum(before, axis=1, dtype=jnp.int32) + jnp.where(
        mine_moving, ROWS - jnp.sum(mine_moving, dtype=jnp.int32), 0
    )
    at = rank[None, :] == local_ids[:, None]
    order = chosen(at, local_ids[None, :])
    length = chosen(at, tool_length[None, :])
    row_of = chosen(at, mine_row[None, :])

    place = jnp.stack([x, zh]).astype(jnp.int32)
    b = lax.dynamic_index_in_dim(write_basis, x, 2, keepdims=False)
    cc = lax.dynamic_index_in_dim(read_basis, x, 2, keepdims=False)
    dt = step_raw.reshape(ROWS, 4, 128)
    par = jnp.repeat(jnp.stack([step_bias, decay_rate, skip_gain]), 64, axis=1).reshape(3, 4, 128)
    gain = norm_gain.reshape(1, 512)

    def sums_of(sq):
        return (sq, shift(sq, "zh", 1), shift(sq, "zh", 2), shift(sq, "zh", 3))

    def reduce_over(gated, sums):
        received = []
        for step in (2, 1, 3):
            part = project(place, step, gated, sums, gain, out_weight)
            received.append(shift(part, "x", step))
        zs = own_project(place, gated, sums, gain, out_weight, received)
        return [zs[0]] + [shift(zs[k], "zh", k) for k in (1, 2, 3)]

    table1 = jnp.concatenate(
        [order[:HALF], length[:HALF], jnp.zeros((HALF,), jnp.int32), row_of[:HALF]]
    )
    gated1, sq1, states1 = run_ssm(
        table1, ssm_input, gate_input, b, cc, dt, par, [ssm_states], None
    )
    sums1 = sums_of(sq1)
    parts1 = reduce_over(gated1, sums1)

    beside_across = shift(across, "c", 1)
    plane = [buf, across, beside, beside_across]
    plane_of = source // 4
    spot = ((source // 2) % 2 ^ zl) + 2 * ((source % 2) ^ c)
    same_plane = (
        moving[None, :]
        & (dest[None, :] == dest[:, None])
        & (plane_of[None, :] == plane_of[:, None])
        & earlier
    )
    plane_slot = jnp.sum(same_plane, axis=1, dtype=jnp.int32)
    steps = jnp.arange(1, 4, dtype=jnp.int32)
    targets = (((y + steps) % 4) * 2 + zl) * 2 + c
    going = moving & (plane_of == y)
    wanted = (
        going[None, None, :]
        & (dest[None, None, :] == targets[:, None, None])
        & (plane_slot[None, None, :] == slots[None, :, None])
    )
    pick_table = jnp.concatenate(
        [
            chosen(wanted, spot[None, None, :]).reshape(-1),
            chosen(wanted, leave_slot[None, None, :]).reshape(-1),
        ]
    )
    sends = pick(pick_table, plane)
    arrived = [shift(sends[k], "y", k + 1) for k in range(3)]

    mine = lambda v: lax.dynamic_slice_in_dim(v, lo, ROWS)
    hops = (y - mine(plane_of)) % 4
    code = jnp.where(
        mine_moving, jnp.where(hops == 0, 1 + mine(spot), 4 + hops), 0
    )
    index = jnp.where(
        mine_moving, jnp.where(hops == 0, mine(leave_slot), mine(plane_slot)), mine_row
    )
    code2 = chosen(at, code[None, :])[HALF:]
    index2 = chosen(at, index[None, :])[HALF:]
    per_source = jnp.where(
        jnp.arange(8, dtype=jnp.int32)[:, None] == code2[None, :], index2[None, :], 0
    )
    table2 = jnp.concatenate([order[HALF:], length[HALF:], code2, per_source.reshape(-1)])
    gated2, sq2, new_states = run_ssm(
        table2,
        ssm_input,
        gate_input,
        b,
        cc,
        dt,
        par,
        [ssm_states, *plane, *arrived],
        states1,
    )
    sums2 = sums_of(sq2)
    parts2 = reduce_over(gated2, sums2)
    half_out = finish(order[:HALF], parts1, None)
    layer_out = finish(order[HALF:], parts2, half_out)
    return layer_out, new_states


def solution(mesh):
    fine = Mesh(mesh.devices.reshape(4, 2, 2, 4, 4), ("y", "zl", "c", "x", "zh"))
    dp, tp = ("y", "zl", "c"), ("x", "zh")
    placed = (
        P(dp, None, tp),
        P(dp, None, tp),
        P(dp, None, None, None),
        P(dp, None, None, None),
        P(dp, tp, None),
        P(tp),
        P(tp),
        P(tp),
        P(tp),
        P(tp, None),
        P(dp, tp, None, None),
        P(),
        P(dp),
    )
    return jax.shard_map(
        local,
        mesh=fine,
        in_specs=placed,
        out_specs=(P(dp, None, tp), P(dp, tp, None, None)),
        check_vma=False,
    )
```

```python
import functools
import jax
import jax.numpy as jnp
import numpy as np
from jax import lax
from jax.experimental import pallas as pl
from jax.experimental.pallas import tpu as pltpu
from jax.sharding import Mesh, PartitionSpec as P

F32 = jnp.float32
BF16 = jnp.bfloat16
SIZES = {"y": 4, "zl": 2, "c": 2, "x": 4, "zh": 4}
ROWS = 8
HALF = 4
NEW = 64
NT = (((1,), (1,)), ((), ()))
TN = (((0,), (0,)), ((), ()))
LIMIT = pltpu.CompilerParams(vmem_limit_bytes=16 << 20)
WIDE = pltpu.CompilerParams(vmem_limit_bytes=57 << 20)
FREE = pl.CostEstimate(flops=0, bytes_accessed=0, transcendentals=0)
ANYWHERE = pl.BlockSpec(memory_space=pl.ANY)
STATE = (1, 8, 64, 128)

LEAVE, ORDER, LENGTH, CODE, INDEX = 0, 8, 16, 24, 32
BESIDE, BESIDE_ROW, ACROSS, ACROSS_ROW = 40, 48, 56, 64
X_AT, C_AT, ZH_AT = 72, 73, 74


def shift(value, axis, step):
    size = SIZES[axis]
    return lax.ppermute(value, axis, [(i, (i + step) % size) for i in range(size)])


def flip(value, mask):
    return lax.ppermute(value, "x", [(i, i ^ mask) for i in range(4)])


def route_kernel(place, lengths, anchor, out):
    y, zl, c, x, zh = (place[k] for k in range(5))
    me = (y * 2 + zl) * 2 + c
    lane = lax.broadcasted_iota(jnp.int32, (128, 128), 1)
    sub = lax.broadcasted_iota(jnp.int32, (128, 128), 0)
    here = jnp.broadcast_to(anchor[...].astype(F32), (128, 128))
    a_i = here.astype(jnp.int32)
    a_j = jnp.transpose(here).astype(jnp.int32)
    one = lambda mask: jnp.where(mask, 1, 0)
    earlier = one(sub < lane)
    same_dest = one((sub >> 3) == (lane >> 3))
    moves_i = one((a_i >> 3) != (lane >> 3))
    moves_j = one((a_j >> 3) != (sub >> 3))
    total = lambda m: jnp.sum(m.astype(F32), axis=0, keepdims=True).astype(jnp.int32)
    leave_slot = total(moves_j * one((a_j >> 3) == (a_i >> 3)) * earlier)
    before = moves_j * same_dest * earlier
    column_slot = total(before * one(((a_j >> 3) & 3) == ((a_i >> 3) & 3)))
    side_slot = total(before * one(((a_j >> 4) & 1) == ((a_i >> 4) & 1)))
    alike = one(moves_j == moves_i) * earlier
    rank = total(same_dest * (alike + moves_i * (1 - moves_j)))

    row = lambda v: jnp.broadcast_to(v, (8, 128))
    lane8 = lax.broadcasted_iota(jnp.int32, (8, 128), 1)
    q = lax.broadcasted_iota(jnp.int32, (8, 128), 0)
    a8 = row(a_i[0:1])
    leave8, column8, side8, rank8 = row(leave_slot), row(column_slot), row(side_slot), row(rank)
    source = a8 >> 3
    dest = lane8 >> 3
    moving = one(source != dest)
    source_row = a8 & 7
    hops = ((dest >> 2) - (source >> 2)) & 3
    same_zl = one(((source ^ dest) & 2) == 0)
    same_c = one(((source ^ dest) & 1) == 0)
    pick = lambda mask, yes, no: jnp.where(mask == 1, yes, no)
    code = moving * pick(same_zl, pick(same_c, 1 + hops, 5), 6)
    index = pick(
        moving, pick(same_zl, pick(same_c, leave8, column8), side8), source_row
    )
    length8 = jnp.zeros((8, 128), jnp.int32)
    for j in range(ROWS):
        length8 = jnp.where((lane8 & 7) == j, lengths[j], length8)
    take = lambda mask, value: jnp.sum((mask * value).astype(F32), axis=1, keepdims=True)
    leaving = moving * one(source == me) * one(leave8 == q)
    mine = one(dest == me) * one(rank8 == q)
    target = jnp.where(q < 4, (y * 2 + zl) * 2, (y * 2 + 1 - zl) * 2) + 1 - c
    beside = moving * one((source & 3) == zl * 2 + c) * one(dest == target)
    beside = beside * one(column8 == (q & 3))
    across = moving * one(((source >> 1) & 1) == zl) * one(dest == (y * 2 + 1 - zl) * 2 + c)
    across = across * one(side8 == q)
    own_column = one((source & 1) == c)
    parts = [
        take(leaving, source_row),
        take(mine, lane8 & 7),
        take(mine, length8),
        take(mine, code),
        take(mine, index),
        take(beside, hops),
        take(beside, leave8),
        take(across, pick(own_column, hops, 4)),
        take(across, pick(own_column, leave8, 4 + column8)),
    ]
    at = q[:, 0:1]
    tail = jnp.where(at == 0, x, jnp.where(at == 1, c, jnp.where(at == 2, zh, 0))).astype(F32)
    parts.append(tail)
    parts.append(jnp.zeros((128 - 8 * len(parts), 1), F32))
    column = jnp.concatenate(parts, axis=0)
    table = jnp.transpose(jnp.broadcast_to(column, (128, 128)))
    out[...] = table[0:1].astype(jnp.int32)


def route(place, tool_length, anchor):
    smem = pl.BlockSpec(memory_space=pltpu.SMEM)
    table = pl.pallas_call(
        route_kernel,
        in_specs=[smem, smem, pl.BlockSpec(memory_space=pltpu.VMEM)],
        out_specs=pl.BlockSpec(memory_space=pltpu.VMEM),
        out_shape=jax.ShapeDtypeStruct((1, 128), jnp.int32),
        compiler_params=LIMIT,
        cost_estimate=FREE,
        name="route",
    )(place, tool_length, anchor.reshape(1, 128))
    return table.reshape(128)


def per_head(ref):
    first = lax.broadcasted_iota(jnp.int32, (1, 128), 1) < 64
    return jnp.concatenate([jnp.where(first, ref[2 * p], ref[2 * p + 1]) for p in range(4)], axis=0)


def fly(value):
    near = lax.ppermute(value, "zh", [(i, i ^ 1) for i in range(4)])
    half = value + near
    return [half, lax.ppermute(half, "zh", [(i, i ^ 3) for i in range(4)])]


def product(left, right):
    return jnp.dot(left, right, preferred_element_type=F32)


def thirds(value):
    parts = []
    for _ in range(3):
        parts.append(value.astype(BF16))
        value = value - parts[-1].astype(F32)
    return parts


def ssm_kernel(start, count, unused, sc, x_ref, g_ref, b_ref, c_ref, dt_ref, bias, rate, skip, *refs):
    sources, refs = refs[:count], refs[count + unused :]
    gated_ref, sq_ref, new_ref, s_all, sems = refs
    r = pl.program_id(0)
    length = sc[LENGTH + start + r]

    @pl.when(r == 0)
    def _():
        for k in range(HALF):
            for which, source in enumerate(sources):

                @pl.when(sc[CODE + start + k] == which)
                def _():
                    pltpu.make_async_copy(
                        source.at[sc[INDEX + start + k]], s_all.at[k], sems.at[k]
                    ).start()

    pltpu.make_async_copy(sources[0].at[0], s_all.at[r], sems.at[r]).wait()
    held = s_all.at[r]
    lane = lax.broadcasted_iota(jnp.int32, (NEW, 128), 1)
    sub = lax.broadcasted_iota(jnp.int32, (NEW, 128), 0)
    within = lane & 63
    causal = within <= sub
    eye = within == sub
    first_half = lane < 64
    live = sub < length
    rows = lax.broadcasted_iota(jnp.int32, (128, 128), 0)
    cols = lax.broadcasted_iota(jnp.int32, (128, 128), 1)
    same = (rows >> 6) == (cols >> 6)
    same_head = jnp.where(same, 1.0, 0.0).astype(BF16)
    upper = jnp.where(same & (rows <= cols), 1.0, 0.0).astype(BF16)
    bias4, rate4, skip4 = per_head(bias), per_head(rate), per_head(skip)
    steps = dt_ref[0]
    raw = bias4 + jnp.concatenate(
        [
            jnp.concatenate([steps[2 * p : 2 * p + 1], steps[2 * p + 1 : 2 * p + 2]], axis=1)
            for p in range(4)
        ],
        axis=0,
    )
    soft = jnp.maximum(raw, 0.0) + jnp.log1p(jnp.exp(-jnp.abs(raw)))
    lane4 = lax.broadcasted_iota(jnp.int32, (4, 128), 1) & 63
    dt4 = jnp.where(lane4 < length, soft, 0.0)
    a4 = -rate4 * dt4
    pieces = [jnp.where(causal, a4[p : p + 1], 0.0) for p in range(4)]
    pieces += [jnp.where(eye, dt4[p : p + 1], 0.0) for p in range(4)]
    spread = sum(product(part, same_head) for part in thirds(jnp.concatenate(pieces, axis=0)))
    stacked = jnp.concatenate([part.astype(F32) for part in thirds(a4)] + [a4 * 0.0], axis=0)
    both = product(stacked.astype(BF16), jnp.concatenate([upper, same_head], axis=1))
    both = both[0:4] + both[4:8] + both[8:12]
    ds4, tot4 = both[:, :128], both[:, 128:]
    wide = lax.broadcasted_iota(jnp.int32, (NEW, 4 * NEW), 1)
    tall = lax.broadcasted_iota(jnp.int32, (NEW, 4 * NEW), 0)
    group = jnp.where(wide == 4 * tall + sc[X_AT], 1.0, 0.0).astype(BF16)
    c_val = jnp.dot(group, c_ref[0], preferred_element_type=F32).astype(BF16)
    b_val = jnp.dot(group, b_ref[0], preferred_element_type=F32).astype(BF16)
    bb = jnp.concatenate([b_val, b_val], axis=0)
    affinity = lax.dot_general(c_val, bb, NT, preferred_element_type=F32)
    affinity = jnp.where(causal, affinity, 0.0)
    squares = jnp.zeros((NEW, 128), F32)
    for p in range(4):
        ds_t = spread[p * NEW : (p + 1) * NEW]
        dt_t = spread[(4 + p) * NEW : (5 + p) * NEW]
        mix = affinity * jnp.exp(ds_t - ds4[p : p + 1]) * dt4[p : p + 1]
        hi = mix.astype(BF16)
        lo = (mix - hi.astype(F32)).astype(BF16)
        xf = x_ref[0, :, p * 128 : (p + 1) * 128].astype(F32)
        blocks = jnp.concatenate(
            [jnp.where(first_half, xf, 0.0), jnp.where(first_half, 0.0, xf)], axis=0
        ).astype(BF16)
        inner = jnp.dot(hi, blocks, preferred_element_type=F32) + jnp.dot(
            lo, blocks, preferred_element_type=F32
        )
        state = held[2 * p : 2 * p + 2].reshape(128, 128)
        carried = lax.dot_general(c_val, state, NT, preferred_element_type=F32)
        out = inner + carried * jnp.exp(ds_t) + skip4[p : p + 1] * xf
        gf = g_ref[0, :, p * 128 : (p + 1) * 128].astype(F32)
        gated = jnp.where(live, out * (gf / (1.0 + jnp.exp(-gf))), 0.0)
        gated_ref[0, :, p * 128 : (p + 1) * 128] = gated
        squares = squares + gated * gated
        weighted = xf * (jnp.exp(tot4[p : p + 1] - ds_t) * dt_t)
        w_hi = weighted.astype(BF16)
        w_lo = (weighted - w_hi.astype(F32)).astype(BF16)
        both = jnp.concatenate([w_hi, w_lo], axis=0)
        update = lax.dot_general(both, bb, TN, preferred_element_type=F32)
        e_tot = jnp.exp(tot4[p : p + 1])
        for k in range(2):
            kept = state[k * 64 : (k + 1) * 64].astype(F32) * e_tot[:, k * 64 : k * 64 + 1]
            new_ref[0, 2 * p + k] = (kept + update[k * 64 : (k + 1) * 64]).astype(BF16)
    ones = jnp.ones((8, 128), BF16)
    sq = sum(
        lax.dot_general(ones, part, NT, preferred_element_type=F32) for part in thirds(squares)[:2]
    )
    sq_ref[0] = sq[0:1]


def run_ssm(table, start, x, gate, b, c, dt, scalars, sources, alias, after=()):
    row3 = lambda r, sc: (sc[ORDER + start + r], 0, 0)
    smem = pl.BlockSpec(memory_space=pltpu.SMEM)
    in_specs = [
        pl.BlockSpec((1, NEW, 512), row3),
        pl.BlockSpec((1, NEW, 512), row3),
        pl.BlockSpec((1, 4 * NEW, 128), row3),
        pl.BlockSpec((1, 4 * NEW, 128), row3),
        pl.BlockSpec((1, 8, NEW), row3),
        *[smem] * 3,
        *[ANYWHERE] * (len(sources) + len(after)),
    ]
    operands = [table, x, gate, b, c, dt, *scalars, *sources, *after]
    unused = len(after)
    aliases = {}
    if alias is not None:
        in_specs.append(ANYWHERE)
        aliases = {len(operands): 2}
        operands.append(alias)
        unused += 1
    return pl.pallas_call(
        functools.partial(ssm_kernel, start, len(sources), unused),
        grid_spec=pltpu.PrefetchScalarGridSpec(
            num_scalar_prefetch=1,
            grid=(HALF,),
            in_specs=in_specs,
            out_specs=[
                pl.BlockSpec((1, NEW, 512), lambda r, sc: (r, 0, 0)),
                pl.BlockSpec((1, 1, NEW), lambda r, sc: (r, 0, 0)),
                pl.BlockSpec(STATE, lambda r, sc: (sc[ORDER + start + r], 0, 0, 0)),
            ],
            scratch_shapes=[
                pltpu.VMEM((HALF, 8, 64, 128), BF16),
                pltpu.SemaphoreType.DMA((HALF,)),
            ],
        ),
        out_shape=[
            jax.ShapeDtypeStruct((HALF, NEW, 512), F32),
            jax.ShapeDtypeStruct((HALF, 1, NEW), F32),
            jax.ShapeDtypeStruct((ROWS, 8, 64, 128), BF16),
        ],
        input_output_aliases=aliases,
        compiler_params=LIMIT,
        cost_estimate=FREE,
        name="ssm",
    )(*operands)


def normalise_kernel(count, gated, *refs):
    sums, (gain, after, out) = refs[:count], refs[count:]
    rows = lax.broadcasted_iota(jnp.int32, (NEW, NEW), 0)
    cols = lax.broadcasted_iota(jnp.int32, (NEW, NEW), 1)
    for r in range(HALF):
        total = sum(part[r] for part in sums)
        scale = lax.rsqrt(total / 2048.0 + 1e-05)
        column = jnp.sum(jnp.where(rows == cols, scale, 0.0), axis=1, keepdims=True)
        out[r * NEW : (r + 1) * NEW] = (gated[r] * column * gain[...]).astype(BF16)


def normalise(gated, sums, gain, after):
    whole = pl.BlockSpec(memory_space=pltpu.VMEM)
    return pl.pallas_call(
        functools.partial(normalise_kernel, len(sums)),
        in_specs=[whole] * (2 + len(sums)) + [ANYWHERE],
        out_specs=whole,
        out_shape=jax.ShapeDtypeStruct((HALF * NEW, 512), BF16),
        compiler_params=LIMIT,
        cost_estimate=FREE,
        name="normalise",
    )(gated, *sums, gain, after)


def project_kernel(sc, a, near0, near1, w0, w1, got, other, after, out0, out1):
    for side, near, w, out in ((0, near0, w0, out0), (1, near1, w1, out1)):

        @pl.when(sc[C_AT] == 1)
        def _():
            out[...] = (product(a[...], w[...]) + product(near[...], got[side])).astype(BF16)

        @pl.when(sc[C_AT] != 1)
        def _():
            out[...] = (product(a[...], w[...]) + product(near[...], other[side])).astype(BF16)


def project(table, a, nears, parts, weights, after):
    rows = HALF * NEW
    whole = pl.BlockSpec(memory_space=pltpu.VMEM)
    return pl.pallas_call(
        project_kernel,
        grid_spec=pltpu.PrefetchScalarGridSpec(
            num_scalar_prefetch=1,
            grid=(1,),
            in_specs=[whole] * 7 + [ANYWHERE],
            out_specs=[whole] * 2,
        ),
        out_shape=[jax.ShapeDtypeStruct((rows, 1024), BF16)] * 2,
        compiler_params=LIMIT,
        cost_estimate=FREE,
        name="project",
    )(table, a, *nears, *parts, *weights, after)


def base_kernel(sc, a, near0, near1, w, got, other, after, out):
    for side, near in ((0, near0), (1, near1)):
        columns = slice(side * 1024, (side + 1) * 1024)

        @pl.when(sc[C_AT] == 0)
        def _():
            out[:, columns] = product(a[...], w[:, columns]) + product(near[...], got[side])

        @pl.when(sc[C_AT] != 0)
        def _():
            out[:, columns] = product(a[...], w[:, columns]) + product(near[...], other[side])


def base_project(table, a, nears, own, weights, after):
    rows = HALF * NEW
    whole = pl.BlockSpec(memory_space=pltpu.VMEM)
    return pl.pallas_call(
        base_kernel,
        grid_spec=pltpu.PrefetchScalarGridSpec(
            num_scalar_prefetch=1,
            grid=(1,),
            in_specs=[whole] * 6 + [ANYWHERE],
            out_specs=whole,
        ),
        out_shape=jax.ShapeDtypeStruct((rows, 2048), F32),
        compiler_params=LIMIT,
        cost_estimate=FREE,
        name="base",
    )(table, a, *nears, own, *weights, after)


def combine_kernel(sc, base, e0, e1, after, z0, z1, z2, z3):
    j = pl.program_id(0)
    arrived = jnp.where((sc[ZH_AT] + j) % 4 < 2, e0[...].astype(F32), e1[...].astype(F32))
    value = base[...] + arrived

    @pl.when(j == 0)
    def _():
        z0[...] = value

    for k, ref in ((1, z1), (2, z2), (3, z3)):

        @pl.when(j == k)
        def _():
            ref[...] = value.astype(BF16)


def combine(table, base, e0, e1, after):
    rows = HALF * NEW
    whole = pl.BlockSpec((rows, 512), lambda j, sc: (0, 0))
    at = lambda j, sc: (sc[ZH_AT] + j) % 4
    return pl.pallas_call(
        combine_kernel,
        grid_spec=pltpu.PrefetchScalarGridSpec(
            num_scalar_prefetch=1,
            grid=(4,),
            in_specs=[
                pl.BlockSpec((rows, 512), lambda j, sc: (0, at(j, sc))),
                pl.BlockSpec((rows, 512), lambda j, sc: (0, jnp.minimum(at(j, sc), 1))),
                pl.BlockSpec((rows, 512), lambda j, sc: (0, jnp.maximum(at(j, sc) - 2, 0))),
                ANYWHERE,
            ],
            out_specs=[whole] * 4,
        ),
        out_shape=[
            jax.ShapeDtypeStruct((rows, 512), F32),
            *[jax.ShapeDtypeStruct((rows, 512), BF16) for _ in range(3)],
        ],
        compiler_params=LIMIT,
        cost_estimate=FREE,
        name="combine",
    )(table, base, e0, e1, after)


def slice_kernel(first, count, sc, *refs):
    w, outs, sems = refs[0], refs[2 : 2 + count], refs[-1]
    x, c = sc[X_AT], sc[C_AT]
    starts = [(x ^ 1 ^ (3 * c)) * 2, (x ^ 3 ^ c) * 2 + 1, (x ^ 3) * 2, (x ^ 1) * 2 + 1, x]
    copies = []
    for k, out in enumerate(outs):
        start = starts[first + k]
        width = out.shape[1]
        columns = pl.ds(pl.multiple_of(start * width, width), width)
        for part in range(4):
            rows = pl.ds(part * 128, 128)
            copies.append(
                pltpu.make_async_copy(w.at[rows, columns], out.at[rows], sems.at[k, part])
            )
            copies[-1].start()
    for copy in copies:
        copy.wait()


def slices(table, w, after, first, last):
    widths = [1024, 1024, 1024, 1024, 2048][first:last]
    return pl.pallas_call(
        functools.partial(slice_kernel, first, len(widths)),
        grid_spec=pltpu.PrefetchScalarGridSpec(
            num_scalar_prefetch=1,
            grid=(1,),
            in_specs=[ANYWHERE] * 2,
            out_specs=[pl.BlockSpec(memory_space=pltpu.VMEM)] * len(widths),
            scratch_shapes=[pltpu.SemaphoreType.DMA((len(widths), 4))],
        ),
        out_shape=[jax.ShapeDtypeStruct((512, width), BF16) for width in widths],
        compiler_params=WIDE,
        cost_estimate=FREE,
        name="slices",
    )(table, w, after)


def hold_kernel(value, after, out):
    pass


def hold(value, after):
    return pl.pallas_call(
        hold_kernel,
        in_specs=[ANYWHERE] * 2,
        out_specs=ANYWHERE,
        out_shape=jax.ShapeDtypeStruct(value.shape, value.dtype),
        input_output_aliases={0: 0},
        compiler_params=LIMIT,
        cost_estimate=FREE,
        name="hold",
    )(value, after)


def join_kernel(first, second, after, out, sems):
    copies = [
        pltpu.make_async_copy(ref, out.at[k], sems.at[k]) for k, ref in enumerate((first, second))
    ]
    for copy in copies:
        copy.start()
    for copy in copies:
        copy.wait()


def join(first, second, after):
    return pl.pallas_call(
        join_kernel,
        in_specs=[ANYWHERE] * 3,
        out_specs=pl.BlockSpec(memory_space=pltpu.VMEM),
        out_shape=jax.ShapeDtypeStruct((2, *first.shape), first.dtype),
        scratch_shapes=[pltpu.SemaphoreType.DMA((2,))],
        compiler_params=LIMIT,
        cost_estimate=FREE,
        name="join",
    )(first, second, after)


def gather_kernel(z0, r1, r3, out):
    out[...] = z0[...] + r1[...].astype(F32) + r3[...].astype(F32)


def gather_sum(z0, r1, r3):
    whole = pl.BlockSpec(memory_space=pltpu.VMEM)
    return pl.pallas_call(
        gather_kernel,
        in_specs=[whole] * 3,
        out_specs=whole,
        out_shape=jax.ShapeDtypeStruct(z0.shape, F32),
        compiler_params=LIMIT,
        cost_estimate=FREE,
        name="gather_sum",
    )(z0, r1, r3)


def finish_kernel(count, first, sc, *refs):
    parts = refs[:count]
    out, held, sem = refs[-3:]
    value = parts[0][...]
    for part in parts[1:]:
        value = value + part[...].astype(F32)
    held[...] = value.astype(BF16)
    copies = [
        pltpu.make_async_copy(
            held.at[pl.ds(r * NEW, NEW)], out.at[sc[ORDER + first + r]], sem.at[r]
        )
        for r in range(HALF)
    ]
    for copy in copies:
        copy.start()
    for copy in copies:
        copy.wait()


def finish(table, parts, first, alias):
    whole = pl.BlockSpec(memory_space=pltpu.VMEM)
    in_specs = [whole] * len(parts)
    operands = [table, *parts]
    aliases = {}
    if alias is not None:
        in_specs.append(ANYWHERE)
        aliases = {len(operands): 0}
        operands.append(alias)
    return pl.pallas_call(
        functools.partial(finish_kernel, len(parts), first),
        grid_spec=pltpu.PrefetchScalarGridSpec(
            num_scalar_prefetch=1,
            grid=(1,),
            in_specs=in_specs,
            out_specs=ANYWHERE,
            scratch_shapes=[
                pltpu.VMEM((HALF * NEW, 512), BF16),
                pltpu.SemaphoreType.DMA((HALF,)),
            ],
        ),
        out_shape=jax.ShapeDtypeStruct((ROWS, NEW, 512), BF16),
        input_output_aliases=aliases,
        compiler_params=LIMIT,
        cost_estimate=FREE,
        name="finish",
    )(*operands)


def copy_kernel(sc, source, out):
    out[...] = source[...]


def leave(table, states):
    return pl.pallas_call(
        copy_kernel,
        grid_spec=pltpu.PrefetchScalarGridSpec(
            num_scalar_prefetch=1,
            grid=(HALF,),
            in_specs=[pl.BlockSpec(STATE, lambda q, sc: (sc[LEAVE + q], 0, 0, 0))],
            out_specs=pl.BlockSpec(STATE, lambda q, sc: (q, 0, 0, 0)),
        ),
        out_shape=jax.ShapeDtypeStruct((HALF, 8, 64, 128), BF16),
        compiler_params=LIMIT,
        cost_estimate=FREE,
        name="leave",
    )(table, states)


def pick_kernel(count, start, start_row, sc, *refs):
    sources, out, sems = refs[:count], refs[-2], refs[-1]
    slots = out.shape[0]
    for q in range(slots):
        for which in range(count):

            @pl.when(sc[start + q] == which)
            def _():
                row = sc[start_row + q]
                pltpu.make_async_copy(sources[which].at[row], out.at[q], sems.at[q]).start()

    for q in range(slots):
        pltpu.make_async_copy(sources[0].at[0], out.at[q], sems.at[q]).wait()


def pick(table, sources, start, start_row, slots, after):
    return pl.pallas_call(
        functools.partial(pick_kernel, len(sources), start, start_row),
        grid_spec=pltpu.PrefetchScalarGridSpec(
            num_scalar_prefetch=1,
            grid=(1,),
            in_specs=[ANYWHERE] * (len(sources) + 1),
            out_specs=pl.BlockSpec(memory_space=pltpu.VMEM),
            scratch_shapes=[pltpu.SemaphoreType.DMA((slots,))],
        ),
        out_shape=jax.ShapeDtypeStruct((slots, 8, 64, 128), BF16),
        compiler_params=LIMIT,
        cost_estimate=FREE,
        name="pick",
    )(table, *sources, after)


def local(
    ssm_input,
    gate_input,
    write_basis,
    read_basis,
    step_raw,
    step_bias,
    decay_rate,
    skip_gain,
    norm_gain,
    out_weight,
    ssm_states,
    anchor,
    tool_length,
):
    place = jnp.stack([lax.axis_index(n) for n in ("y", "zl", "c", "x", "zh")]).astype(jnp.int32)
    table = route(place, tool_length, anchor)
    buf = leave(table, ssm_states)
    along = [buf] + [shift(buf, "y", k) for k in (1, 2, 3)]

    shares = slices(table, out_weight, buf, 0, 2)
    got = [flip(shares[0], 1), flip(shares[1], 3)]

    b = write_basis.reshape(ROWS, 4 * NEW, 128)
    c = read_basis.reshape(ROWS, 4 * NEW, 128)
    gain = norm_gain.reshape(1, 512)
    ssm = functools.partial(
        run_ssm,
        table,
        x=ssm_input,
        gate=gate_input,
        b=b,
        c=c,
        dt=step_raw,
        scalars=(step_bias, decay_rate, skip_gain),
    )

    def spread_rows(gated, sums, after):
        a = normalise(gated, sums, gain, after)
        return a, [flip(a, 1), flip(a, 3)]

    def reduce_rest(base, moved, after):
        zs = combine(table, base, *moved, after)
        return [zs[0]] + [shift(zs[k], "zh", k) for k in (1, 2, 3)]

    gated1, sq1, states1 = ssm(start=0, sources=[ssm_states], alias=None, after=[shares[0]])
    sums1 = lax.psum(sq1, "zh")

    part0, part1, own = slices(table, out_weight, sums1, 2, 5)
    chosen = pick(table, along, BESIDE, BESIDE_ROW, 8, own)
    beside = shift(chosen, "c", 1)
    near_weights = join(*got, chosen)
    a1, nears1 = spread_rows(gated1, [sums1], near_weights)
    picked = pick(table, [*along, beside], ACROSS, ACROSS_ROW, HALF, a1)
    across = shift(picked, "zl", 1)
    near_weights = hold(near_weights, picked)
    weights = [near_weights, shift(near_weights, "c", 1)]
    sent1 = project(table, a1, nears1, [part0, part1], weights, picked)
    moved1 = [flip(sent1[0], 3), flip(sent1[1], 1)]
    base1 = base_project(table, a1, nears1, own, weights, sent1[0])

    gated2, sq2, new_states = ssm(
        start=HALF, sources=[ssm_states, *along, beside, across], alias=states1, after=[sent1[0]]
    )
    sums2 = fly(sq2)
    z0, r1, r2, r3 = reduce_rest(base1, moved1, sq2)
    a2, nears2 = spread_rows(gated2, sums2, z0)
    gathered = gather_sum(z0, r1, r3)
    sent2 = project(table, a2, nears2, [part0, part1], weights, gathered)
    moved2 = [flip(sent2[0], 3), flip(sent2[1], 1)]
    base2 = base_project(table, a2, nears2, own, weights, sent2[0])
    half_out = finish(table, [gathered, r2], 0, None)
    done2 = reduce_rest(base2, moved2, half_out)
    return finish(table, done2, HALF, half_out), new_states


def solution(mesh):
    fine = Mesh(mesh.devices.reshape(4, 2, 2, 4, 4), ("y", "zl", "c", "x", "zh"))
    dp, tp = ("y", "zl", "c"), ("x", "zh")
    placed = (
        P(dp, None, tp),
        P(dp, None, tp),
        P(dp, None, None, None),
        P(dp, None, None, None),
        P(dp, tp, None),
        P(tp),
        P(tp),
        P(tp),
        P(tp),
        P(tp, None),
        P(dp, tp, None, None),
        P(),
        P(dp),
    )
    return jax.shard_map(
        local,
        mesh=fine,
        in_specs=placed,
        out_specs=(P(dp, None, tp), P(dp, tp, None, None)),
        check_vma=False,
    )
```

```python
import functools
import jax
import jax.numpy as jnp
import numpy as np
from jax import lax
from jax.experimental import pallas as pl
from jax.experimental.pallas import tpu as pltpu
from jax.sharding import Mesh, PartitionSpec as P

F32 = jnp.float32
BF16 = jnp.bfloat16
SIZES = {"y": 4, "zl": 2, "c": 2, "x": 4, "zh": 4}
ROWS = 8
HALF = 4
NEW = 64
NT = (((1,), (1,)), ((), ()))
TN = (((0,), (0,)), ((), ()))
LIMIT = pltpu.CompilerParams(vmem_limit_bytes=16 << 20)
WIDE = pltpu.CompilerParams(vmem_limit_bytes=57 << 20)
FREE = pl.CostEstimate(flops=0, bytes_accessed=0, transcendentals=0)
ANYWHERE = pl.BlockSpec(memory_space=pl.ANY)
STATE = (1, 8, 64, 128)

LEAVE, ORDER, LENGTH, CODE, INDEX = 0, 8, 16, 24, 32
BESIDE, BESIDE_ROW, ACROSS, ACROSS_ROW = 40, 48, 56, 64
X_AT, C_AT, ZH_AT = 72, 73, 74


def shift(value, axis, step):
    size = SIZES[axis]
    return lax.ppermute(value, axis, [(i, (i + step) % size) for i in range(size)])


def flip(value, mask):
    return lax.ppermute(value, "x", [(i, i ^ mask) for i in range(4)])


def route_kernel(place, lengths, anchor, out):
    y, zl, c, x, zh = (place[k] for k in range(5))
    me = (y * 2 + zl) * 2 + c
    lane = lax.broadcasted_iota(jnp.int32, (128, 128), 1)
    sub = lax.broadcasted_iota(jnp.int32, (128, 128), 0)
    here = jnp.broadcast_to(anchor[...].astype(F32), (128, 128))
    a_i = here.astype(jnp.int32)
    a_j = jnp.transpose(here).astype(jnp.int32)
    one = lambda mask: jnp.where(mask, 1, 0)
    earlier = one(sub < lane)
    same_dest = one((sub >> 3) == (lane >> 3))
    moves_i = one((a_i >> 3) != (lane >> 3))
    moves_j = one((a_j >> 3) != (sub >> 3))
    total = lambda m: jnp.sum(m.astype(F32), axis=0, keepdims=True).astype(jnp.int32)
    leave_slot = total(moves_j * one((a_j >> 3) == (a_i >> 3)) * earlier)
    before = moves_j * same_dest * earlier
    column_slot = total(before * one(((a_j >> 3) & 3) == ((a_i >> 3) & 3)))
    side_slot = total(before * one(((a_j >> 4) & 1) == ((a_i >> 4) & 1)))
    alike = one(moves_j == moves_i) * earlier
    rank = total(same_dest * (alike + moves_i * (1 - moves_j)))

    row = lambda v: jnp.broadcast_to(v, (8, 128))
    lane8 = lax.broadcasted_iota(jnp.int32, (8, 128), 1)
    q = lax.broadcasted_iota(jnp.int32, (8, 128), 0)
    a8 = row(a_i[0:1])
    leave8, column8, side8, rank8 = row(leave_slot), row(column_slot), row(side_slot), row(rank)
    source = a8 >> 3
    dest = lane8 >> 3
    moving = one(source != dest)
    source_row = a8 & 7
    hops = ((dest >> 2) - (source >> 2)) & 3
    same_zl = one(((source ^ dest) & 2) == 0)
    same_c = one(((source ^ dest) & 1) == 0)
    pick = lambda mask, yes, no: jnp.where(mask == 1, yes, no)
    code = moving * pick(same_zl, pick(same_c, 1 + hops, 5), 6)
    index = pick(
        moving, pick(same_zl, pick(same_c, leave8, column8), side8), source_row
    )
    length8 = jnp.zeros((8, 128), jnp.int32)
    for j in range(ROWS):
        length8 = jnp.where((lane8 & 7) == j, lengths[j], length8)
    take = lambda mask, value: jnp.sum((mask * value).astype(F32), axis=1, keepdims=True)
    leaving = moving * one(source == me) * one(leave8 == q)
    mine = one(dest == me) * one(rank8 == q)
    target = jnp.where(q < 4, (y * 2 + zl) * 2, (y * 2 + 1 - zl) * 2) + 1 - c
    beside = moving * one((source & 3) == zl * 2 + c) * one(dest == target)
    beside = beside * one(column8 == (q & 3))
    across = moving * one(((source >> 1) & 1) == zl) * one(dest == (y * 2 + 1 - zl) * 2 + c)
    across = across * one(side8 == q)
    own_column = one((source & 1) == c)
    parts = [
        take(leaving, source_row),
        take(mine, lane8 & 7),
        take(mine, length8),
        take(mine, code),
        take(mine, index),
        take(beside, hops),
        take(beside, leave8),
        take(across, pick(own_column, hops, 4)),
        take(across, pick(own_column, leave8, 4 + column8)),
    ]
    at = q[:, 0:1]
    tail = jnp.where(at == 0, x, jnp.where(at == 1, c, jnp.where(at == 2, zh, 0))).astype(F32)
    parts.append(tail)
    parts.append(jnp.zeros((128 - 8 * len(parts), 1), F32))
    column = jnp.concatenate(parts, axis=0)
    table = jnp.transpose(jnp.broadcast_to(column, (128, 128)))
    out[...] = table[0:1].astype(jnp.int32)


def route(place, tool_length, anchor):
    smem = pl.BlockSpec(memory_space=pltpu.SMEM)
    table = pl.pallas_call(
        route_kernel,
        in_specs=[smem, smem, pl.BlockSpec(memory_space=pltpu.VMEM)],
        out_specs=pl.BlockSpec(memory_space=pltpu.VMEM),
        out_shape=jax.ShapeDtypeStruct((1, 128), jnp.int32),
        compiler_params=LIMIT,
        cost_estimate=FREE,
        name="route",
    )(place, tool_length, anchor.reshape(1, 128))
    return table.reshape(128)


def per_head(ref):
    first = lax.broadcasted_iota(jnp.int32, (1, 128), 1) < 64
    return jnp.concatenate([jnp.where(first, ref[2 * p], ref[2 * p + 1]) for p in range(4)], axis=0)


def fly(value):
    near = lax.ppermute(value, "zh", [(i, i ^ 1) for i in range(4)])
    half = value + near
    return [half, lax.ppermute(half, "zh", [(i, i ^ 3) for i in range(4)])]


def product(left, right):
    return jnp.dot(left, right, preferred_element_type=F32)


def thirds(value):
    parts = []
    for _ in range(3):
        parts.append(value.astype(BF16))
        value = value - parts[-1].astype(F32)
    return parts


def ssm_kernel(start, count, unused, sc, x_ref, g_ref, b_ref, c_ref, dt_ref, bias, rate, skip, *refs):
    sources, refs = refs[:count], refs[count + unused :]
    gated_ref, sq_ref, new_ref, s_all, sems = refs
    r = pl.program_id(0)
    length = sc[LENGTH + start + r]

    @pl.when(r == 0)
    def _():
        for k in range(HALF):
            for which, source in enumerate(sources):

                @pl.when(sc[CODE + start + k] == which)
                def _():
                    pltpu.make_async_copy(
                        source.at[sc[INDEX + start + k]], s_all.at[k], sems.at[k]
                    ).start()

    pltpu.make_async_copy(sources[0].at[0], s_all.at[r], sems.at[r]).wait()
    held = s_all.at[r]
    lane = lax.broadcasted_iota(jnp.int32, (NEW, 128), 1)
    sub = lax.broadcasted_iota(jnp.int32, (NEW, 128), 0)
    within = lane & 63
    causal = within <= sub
    eye = within == sub
    first_half = lane < 64
    live = sub < length
    rows = lax.broadcasted_iota(jnp.int32, (128, 128), 0)
    cols = lax.broadcasted_iota(jnp.int32, (128, 128), 1)
    same = (rows >> 6) == (cols >> 6)
    same_head = jnp.where(same, 1.0, 0.0).astype(BF16)
    upper = jnp.where(same & (rows <= cols), 1.0, 0.0).astype(BF16)
    bias4, rate4, skip4 = per_head(bias), per_head(rate), per_head(skip)
    steps = dt_ref[0]
    raw = bias4 + jnp.concatenate(
        [
            jnp.concatenate([steps[2 * p : 2 * p + 1], steps[2 * p + 1 : 2 * p + 2]], axis=1)
            for p in range(4)
        ],
        axis=0,
    )
    soft = jnp.maximum(raw, 0.0) + jnp.log1p(jnp.exp(-jnp.abs(raw)))
    lane4 = lax.broadcasted_iota(jnp.int32, (4, 128), 1) & 63
    dt4 = jnp.where(lane4 < length, soft, 0.0)
    a4 = -rate4 * dt4
    pieces = [jnp.where(causal, a4[p : p + 1], 0.0) for p in range(4)]
    pieces += [jnp.where(eye, dt4[p : p + 1], 0.0) for p in range(4)]
    spread = sum(product(part, same_head) for part in thirds(jnp.concatenate(pieces, axis=0)))
    stacked = jnp.concatenate([part.astype(F32) for part in thirds(a4)] + [a4 * 0.0], axis=0)
    both = product(stacked.astype(BF16), jnp.concatenate([upper, same_head], axis=1))
    both = both[0:4] + both[4:8] + both[8:12]
    ds4, tot4 = both[:, :128], both[:, 128:]
    wide = lax.broadcasted_iota(jnp.int32, (NEW, 4 * NEW), 1)
    tall = lax.broadcasted_iota(jnp.int32, (NEW, 4 * NEW), 0)
    group = jnp.where(wide == 4 * tall + sc[X_AT], 1.0, 0.0).astype(BF16)
    c_val = jnp.dot(group, c_ref[0], preferred_element_type=F32).astype(BF16)
    b_val = jnp.dot(group, b_ref[0], preferred_element_type=F32).astype(BF16)
    bb = jnp.concatenate([b_val, b_val], axis=0)
    affinity = lax.dot_general(c_val, bb, NT, preferred_element_type=F32)
    affinity = jnp.where(causal, affinity, 0.0)
    squares = jnp.zeros((NEW, 128), F32)
    for p in range(4):
        ds_t = spread[p * NEW : (p + 1) * NEW]
        dt_t = spread[(4 + p) * NEW : (5 + p) * NEW]
        mix = affinity * jnp.exp(ds_t - ds4[p : p + 1]) * dt4[p : p + 1]
        hi = mix.astype(BF16)
        lo = (mix - hi.astype(F32)).astype(BF16)
        xf = x_ref[0, :, p * 128 : (p + 1) * 128].astype(F32)
        blocks = jnp.concatenate(
            [jnp.where(first_half, xf, 0.0), jnp.where(first_half, 0.0, xf)], axis=0
        ).astype(BF16)
        inner = jnp.dot(hi, blocks, preferred_element_type=F32) + jnp.dot(
            lo, blocks, preferred_element_type=F32
        )
        state = held[2 * p : 2 * p + 2].reshape(128, 128)
        carried = lax.dot_general(c_val, state, NT, preferred_element_type=F32)
        out = inner + carried * jnp.exp(ds_t) + skip4[p : p + 1] * xf
        gf = g_ref[0, :, p * 128 : (p + 1) * 128].astype(F32)
        gated = jnp.where(live, out * (gf / (1.0 + jnp.exp(-gf))), 0.0)
        gated_ref[0, :, p * 128 : (p + 1) * 128] = gated
        squares = squares + gated * gated
        weighted = xf * (jnp.exp(tot4[p : p + 1] - ds_t) * dt_t)
        w_hi = weighted.astype(BF16)
        w_lo = (weighted - w_hi.astype(F32)).astype(BF16)
        both = jnp.concatenate([w_hi, w_lo], axis=0)
        update = lax.dot_general(both, bb, TN, preferred_element_type=F32)
        e_tot = jnp.exp(tot4[p : p + 1])
        for k in range(2):
            kept = state[k * 64 : (k + 1) * 64].astype(F32) * e_tot[:, k * 64 : k * 64 + 1]
            new_ref[0, 2 * p + k] = (kept + update[k * 64 : (k + 1) * 64]).astype(BF16)
    ones = jnp.ones((8, 128), BF16)
    sq = sum(
        lax.dot_general(ones, part, NT, preferred_element_type=F32) for part in thirds(squares)[:2]
    )
    sq_ref[0] = sq[0:1]


def run_ssm(table, start, x, gate, b, c, dt, scalars, sources, alias, after=()):
    row3 = lambda r, sc: (sc[ORDER + start + r], 0, 0)
    smem = pl.BlockSpec(memory_space=pltpu.SMEM)
    in_specs = [
        pl.BlockSpec((1, NEW, 512), row3),
        pl.BlockSpec((1, NEW, 512), row3),
        pl.BlockSpec((1, 4 * NEW, 128), row3),
        pl.BlockSpec((1, 4 * NEW, 128), row3),
        pl.BlockSpec((1, 8, NEW), row3),
        *[smem] * 3,
        *[ANYWHERE] * (len(sources) + len(after)),
    ]
    operands = [table, x, gate, b, c, dt, *scalars, *sources, *after]
    unused = len(after)
    aliases = {}
    if alias is not None:
        in_specs.append(ANYWHERE)
        aliases = {len(operands): 2}
        operands.append(alias)
        unused += 1
    return pl.pallas_call(
        functools.partial(ssm_kernel, start, len(sources), unused),
        grid_spec=pltpu.PrefetchScalarGridSpec(
            num_scalar_prefetch=1,
            grid=(HALF,),
            in_specs=in_specs,
            out_specs=[
                pl.BlockSpec((1, NEW, 512), lambda r, sc: (r, 0, 0)),
                pl.BlockSpec((1, 1, NEW), lambda r, sc: (r, 0, 0)),
                pl.BlockSpec(STATE, lambda r, sc: (sc[ORDER + start + r], 0, 0, 0)),
            ],
            scratch_shapes=[
                pltpu.VMEM((HALF, 8, 64, 128), BF16),
                pltpu.SemaphoreType.DMA((HALF,)),
            ],
        ),
        out_shape=[
            jax.ShapeDtypeStruct((HALF, NEW, 512), F32),
            jax.ShapeDtypeStruct((HALF, 1, NEW), F32),
            jax.ShapeDtypeStruct((ROWS, 8, 64, 128), BF16),
        ],
        input_output_aliases=aliases,
        compiler_params=LIMIT,
        cost_estimate=FREE,
        name="ssm",
    )(*operands)


def normalise_kernel(count, gated, *refs):
    sums, (gain, after, out) = refs[:count], refs[count:]
    rows = lax.broadcasted_iota(jnp.int32, (NEW, NEW), 0)
    cols = lax.broadcasted_iota(jnp.int32, (NEW, NEW), 1)
    for r in range(HALF):
        total = sum(part[r] for part in sums)
        scale = lax.rsqrt(total / 2048.0 + 1e-05)
        column = jnp.sum(jnp.where(rows == cols, scale, 0.0), axis=1, keepdims=True)
        out[r * NEW : (r + 1) * NEW] = (gated[r] * column * gain[...]).astype(BF16)


def normalise(gated, sums, gain, after):
    whole = pl.BlockSpec(memory_space=pltpu.VMEM)
    return pl.pallas_call(
        functools.partial(normalise_kernel, len(sums)),
        in_specs=[whole] * (2 + len(sums)) + [ANYWHERE],
        out_specs=whole,
        out_shape=jax.ShapeDtypeStruct((HALF * NEW, 512), BF16),
        compiler_params=LIMIT,
        cost_estimate=FREE,
        name="normalise",
    )(gated, *sums, gain, after)


def project_kernel(sc, a, near0, near1, w0, w1, got, other, after, *outs):
    count = len(outs) // 2
    rows = a.shape[0] // count

    def store(side, value):
        for k in range(count):
            outs[side * count + k][...] = value[k * rows : (k + 1) * rows].astype(BF16)

    for side, near, w in ((0, near0, w0), (1, near1, w1)):

        @pl.when(sc[C_AT] == 1)
        def _():
            store(side, product(a[...], w[...]) + product(near[...], got[side]))

        @pl.when(sc[C_AT] != 1)
        def _():
            store(side, product(a[...], w[...]) + product(near[...], other[side]))


def project(table, a, nears, parts, weights, after, count=1):
    rows = HALF * NEW
    whole = pl.BlockSpec(memory_space=pltpu.VMEM)
    return pl.pallas_call(
        project_kernel,
        grid_spec=pltpu.PrefetchScalarGridSpec(
            num_scalar_prefetch=1,
            grid=(1,),
            in_specs=[whole] * 7 + [ANYWHERE],
            out_specs=[whole] * (2 * count),
        ),
        out_shape=[jax.ShapeDtypeStruct((rows // count, 1024), BF16)] * (2 * count),
        compiler_params=LIMIT,
        cost_estimate=FREE,
        name="project",
    )(table, a, *nears, *parts, *weights, after)


def base_kernel(sc, a, near0, near1, w, got, other, after, out):
    for side, near in ((0, near0), (1, near1)):
        columns = slice(side * 1024, (side + 1) * 1024)

        @pl.when(sc[C_AT] == 0)
        def _():
            out[:, columns] = product(a[...], w[:, columns]) + product(near[...], got[side])

        @pl.when(sc[C_AT] != 0)
        def _():
            out[:, columns] = product(a[...], w[:, columns]) + product(near[...], other[side])


def base_project(table, a, nears, own, weights, after):
    rows = HALF * NEW
    whole = pl.BlockSpec(memory_space=pltpu.VMEM)
    return pl.pallas_call(
        base_kernel,
        grid_spec=pltpu.PrefetchScalarGridSpec(
            num_scalar_prefetch=1,
            grid=(1,),
            in_specs=[whole] * 6 + [ANYWHERE],
            out_specs=whole,
        ),
        out_shape=jax.ShapeDtypeStruct((rows, 2048), F32),
        compiler_params=LIMIT,
        cost_estimate=FREE,
        name="base",
    )(table, a, *nears, own, *weights, after)


def combine_kernel(sc, base, e0, e1, *refs):
    z0, z1, z2, z3 = refs[-4:]
    j = pl.program_id(0)
    arrived = jnp.where((sc[ZH_AT] + j) % 4 < 2, e0[...].astype(F32), e1[...].astype(F32))
    value = base[...] + arrived

    @pl.when(j == 0)
    def _():
        z0[...] = value

    for k, ref in ((1, z1), (2, z2), (3, z3)):

        @pl.when(j == k)
        def _():
            ref[...] = value.astype(BF16)


def combine(table, base, e0, e1, after, part=0):
    rows = e0.shape[0]
    whole = pl.BlockSpec((rows, 512), lambda j, sc: (0, 0))
    at = lambda j, sc: (sc[ZH_AT] + j) % 4
    return pl.pallas_call(
        combine_kernel,
        grid_spec=pltpu.PrefetchScalarGridSpec(
            num_scalar_prefetch=1,
            grid=(4,),
            in_specs=[
                pl.BlockSpec((rows, 512), lambda j, sc: (part, at(j, sc))),
                pl.BlockSpec((rows, 512), lambda j, sc: (0, jnp.minimum(at(j, sc), 1))),
                pl.BlockSpec((rows, 512), lambda j, sc: (0, jnp.maximum(at(j, sc) - 2, 0))),
                *[ANYWHERE] * len(after),
            ],
            out_specs=[whole] * 4,
        ),
        out_shape=[
            jax.ShapeDtypeStruct((rows, 512), F32),
            *[jax.ShapeDtypeStruct((rows, 512), BF16) for _ in range(3)],
        ],
        compiler_params=LIMIT,
        cost_estimate=FREE,
        name="combine",
    )(table, base, e0, e1, *after)


def slice_kernel(first, count, sc, *refs):
    w, outs, sems = refs[0], refs[2 : 2 + count], refs[-1]
    x, c = sc[X_AT], sc[C_AT]
    starts = [(x ^ 1 ^ (3 * c)) * 2, (x ^ 3 ^ c) * 2 + 1, (x ^ 3) * 2, (x ^ 1) * 2 + 1, x]
    copies = []
    for k, out in enumerate(outs):
        start = starts[first + k]
        width = out.shape[1]
        columns = pl.ds(pl.multiple_of(start * width, width), width)
        for part in range(4):
            rows = pl.ds(part * 128, 128)
            copies.append(
                pltpu.make_async_copy(w.at[rows, columns], out.at[rows], sems.at[k, part])
            )
            copies[-1].start()
    for copy in copies:
        copy.wait()


def slices(table, w, after, first, last):
    widths = [1024, 1024, 1024, 1024, 2048][first:last]
    return pl.pallas_call(
        functools.partial(slice_kernel, first, len(widths)),
        grid_spec=pltpu.PrefetchScalarGridSpec(
            num_scalar_prefetch=1,
            grid=(1,),
            in_specs=[ANYWHERE] * 2,
            out_specs=[pl.BlockSpec(memory_space=pltpu.VMEM)] * len(widths),
            scratch_shapes=[pltpu.SemaphoreType.DMA((len(widths), 4))],
        ),
        out_shape=[jax.ShapeDtypeStruct((512, width), BF16) for width in widths],
        compiler_params=WIDE,
        cost_estimate=FREE,
        name="slices",
    )(table, w, after)


def wait_kernel(after, out):
    out[...] = jnp.zeros_like(out)


def wait(after):
    return pl.pallas_call(
        wait_kernel,
        in_specs=[ANYWHERE],
        out_specs=pl.BlockSpec(memory_space=pltpu.VMEM),
        out_shape=jax.ShapeDtypeStruct((8, 128), F32),
        compiler_params=LIMIT,
        cost_estimate=pl.CostEstimate(flops=0, bytes_accessed=16 << 20, transcendentals=0),
        name="wait",
    )(after)


def hold_kernel(value, after, out):
    pass


def hold(value, after):
    return pl.pallas_call(
        hold_kernel,
        in_specs=[ANYWHERE] * 2,
        out_specs=ANYWHERE,
        out_shape=jax.ShapeDtypeStruct(value.shape, value.dtype),
        input_output_aliases={0: 0},
        compiler_params=LIMIT,
        cost_estimate=FREE,
        name="hold",
    )(value, after)


def join_kernel(first, second, after, out, sems):
    copies = [
        pltpu.make_async_copy(ref, out.at[k], sems.at[k]) for k, ref in enumerate((first, second))
    ]
    for copy in copies:
        copy.start()
    for copy in copies:
        copy.wait()


def join(first, second, after):
    return pl.pallas_call(
        join_kernel,
        in_specs=[ANYWHERE] * 3,
        out_specs=pl.BlockSpec(memory_space=pltpu.VMEM),
        out_shape=jax.ShapeDtypeStruct((2, *first.shape), first.dtype),
        scratch_shapes=[pltpu.SemaphoreType.DMA((2,))],
        compiler_params=LIMIT,
        cost_estimate=FREE,
        name="join",
    )(first, second, after)


def gather_kernel(*refs):
    out = refs[-1]
    value = refs[0][...]
    for part in refs[1:-1]:
        value = value + part[...].astype(F32)
    out[...] = value.astype(out.dtype)


def gather_sum(parts, dtype):
    whole = pl.BlockSpec(memory_space=pltpu.VMEM)
    return pl.pallas_call(
        gather_kernel,
        in_specs=[whole] * len(parts),
        out_specs=whole,
        out_shape=jax.ShapeDtypeStruct(parts[0].shape, dtype),
        compiler_params=LIMIT,
        cost_estimate=FREE,
        name="gather_sum",
    )(*parts)


def finish_kernel(sc, half, *refs):
    parts, (out, held, sem) = refs[:-3], refs[-3:]

    def rows_out(source, p):
        rows = pl.ds(p % HALF * NEW, NEW)
        return pltpu.make_async_copy(source.at[rows], out.at[sc[ORDER + p]], sem.at[p])

    copies = [rows_out(half, p) for p in range(HALF)]
    copies += [rows_out(held, p) for p in range(HALF, ROWS)]
    for p in range(HALF):
        copies[p].start()
    at = 0
    for count in 2, 4:
        group, parts = parts[:count], parts[count:]
        value = group[0][...]
        for part in group[1:]:
            value = value + part[...].astype(F32)
        held[at : at + value.shape[0]] = value.astype(BF16)
        at += value.shape[0]
    for p in range(HALF, ROWS):
        copies[p].start()
    for copy in copies:
        copy.wait()


def finish(table, half, parts):
    whole = pl.BlockSpec(memory_space=pltpu.VMEM)
    return pl.pallas_call(
        finish_kernel,
        grid_spec=pltpu.PrefetchScalarGridSpec(
            num_scalar_prefetch=1,
            grid=(1,),
            in_specs=[whole] * (1 + len(parts)),
            out_specs=ANYWHERE,
            scratch_shapes=[
                pltpu.VMEM((HALF * NEW, 512), BF16),
                pltpu.SemaphoreType.DMA((ROWS,)),
            ],
        ),
        out_shape=jax.ShapeDtypeStruct((ROWS, NEW, 512), BF16),
        compiler_params=LIMIT,
        cost_estimate=FREE,
        name="finish",
    )(table, half, *parts)


def copy_kernel(sc, source, out):
    out[...] = source[...]


def leave(table, states):
    return pl.pallas_call(
        copy_kernel,
        grid_spec=pltpu.PrefetchScalarGridSpec(
            num_scalar_prefetch=1,
            grid=(HALF,),
            in_specs=[pl.BlockSpec(STATE, lambda q, sc: (sc[LEAVE + q], 0, 0, 0))],
            out_specs=pl.BlockSpec(STATE, lambda q, sc: (q, 0, 0, 0)),
        ),
        out_shape=jax.ShapeDtypeStruct((HALF, 8, 64, 128), BF16),
        compiler_params=LIMIT,
        cost_estimate=FREE,
        name="leave",
    )(table, states)


def pick_kernel(count, start, start_row, sc, *refs):
    sources, out, sems = refs[:count], refs[-2], refs[-1]
    slots = out.shape[0]
    for q in range(slots):
        for which in range(count):

            @pl.when(sc[start + q] == which)
            def _():
                row = sc[start_row + q]
                pltpu.make_async_copy(sources[which].at[row], out.at[q], sems.at[q]).start()

    for q in range(slots):
        pltpu.make_async_copy(sources[0].at[0], out.at[q], sems.at[q]).wait()


def pick(table, sources, start, start_row, slots, after):
    return pl.pallas_call(
        functools.partial(pick_kernel, len(sources), start, start_row),
        grid_spec=pltpu.PrefetchScalarGridSpec(
            num_scalar_prefetch=1,
            grid=(1,),
            in_specs=[ANYWHERE] * (len(sources) + 1),
            out_specs=pl.BlockSpec(memory_space=pltpu.VMEM),
            scratch_shapes=[pltpu.SemaphoreType.DMA((slots,))],
        ),
        out_shape=jax.ShapeDtypeStruct((slots, 8, 64, 128), BF16),
        compiler_params=LIMIT,
        cost_estimate=FREE,
        name="pick",
    )(table, *sources, after)


def local(
    ssm_input,
    gate_input,
    write_basis,
    read_basis,
    step_raw,
    step_bias,
    decay_rate,
    skip_gain,
    norm_gain,
    out_weight,
    ssm_states,
    anchor,
    tool_length,
):
    place = jnp.stack([lax.axis_index(n) for n in ("y", "zl", "c", "x", "zh")]).astype(jnp.int32)
    table = route(place, tool_length, anchor)
    buf = leave(table, ssm_states)
    along = [buf] + [shift(buf, "y", k) for k in (1, 2, 3)]

    shares = slices(table, out_weight, buf, 0, 2)
    got = [flip(shares[0], 1), flip(shares[1], 3)]
    part0, part1, own = slices(table, out_weight, shares[0], 2, 5)

    b = write_basis.reshape(ROWS, 4 * NEW, 128)
    c = read_basis.reshape(ROWS, 4 * NEW, 128)
    gain = norm_gain.reshape(1, 512)
    ssm = functools.partial(
        run_ssm,
        table,
        x=ssm_input,
        gate=gate_input,
        b=b,
        c=c,
        dt=step_raw,
        scalars=(step_bias, decay_rate, skip_gain),
    )

    def spread_rows(gated, sums, after):
        a = normalise(gated, sums, gain, after)
        return a, [flip(a, 1), flip(a, 3)]

    def reduce_rest(base, moved, after, part=0):
        zs = combine(table, base, *moved, after, part)
        return [zs[0]] + [shift(zs[k], "zh", k) for k in (1, 2, 3)]

    gated1, sq1, states1 = ssm(start=0, sources=[ssm_states], alias=None, after=[own])
    sums1 = lax.psum(sq1, "zh")

    chosen = pick(table, along, BESIDE, BESIDE_ROW, 8, sums1)
    beside = shift(chosen, "c", 1)
    near_weights = join(*got, wait(chosen))
    a1, nears1 = spread_rows(gated1, [sums1], near_weights)
    picked = pick(table, [*along, beside], ACROSS, ACROSS_ROW, HALF, a1)
    across = shift(picked, "zl", 1)
    near_weights = hold(near_weights, picked)
    weights = [near_weights, shift(near_weights, "c", 1)]
    sent1 = project(table, a1, nears1, [part0, part1], weights, picked)
    moved1 = [flip(sent1[0], 3), flip(sent1[1], 1)]
    base1 = base_project(table, a1, nears1, own, weights, sent1[0])

    gated2, sq2, new_states = ssm(
        start=HALF, sources=[ssm_states, *along, beside, across], alias=states1, after=[base1]
    )
    sums2 = fly(sq2)
    z0, r1, r2, r3 = reduce_rest(base1, moved1, [sq2])
    a2, nears2 = spread_rows(gated2, sums2, z0)
    gathered = gather_sum([z0, r1, r3], F32)
    sent2 = project(table, a2, nears2, [part0, part1], weights, gathered, 2)
    moved2 = [[flip(sent2[k], 3), flip(sent2[2 + k], 1)] for k in range(2)]
    base2 = base_project(table, a2, nears2, own, weights, sent2[0])
    z0, r1, late, r3 = reduce_rest(base2, moved2[0], [base2], 0)
    gathered2 = gather_sum([z0, r1, r3], F32)
    half_out = gather_sum([gathered, r2], BF16)
    done2 = reduce_rest(base2, moved2[1], [half_out, gathered2], 1)
    return finish(table, half_out, [gathered2, late, *done2]), new_states


def solution(mesh):
    fine = Mesh(mesh.devices.reshape(4, 2, 2, 4, 4), ("y", "zl", "c", "x", "zh"))
    dp, tp = ("y", "zl", "c"), ("x", "zh")
    placed = (
        P(dp, None, tp),
        P(dp, None, tp),
        P(dp, None, None, None),
        P(dp, None, None, None),
        P(dp, tp, None),
        P(tp),
        P(tp),
        P(tp),
        P(tp),
        P(tp, None),
        P(dp, tp, None, None),
        P(),
        P(dp),
    )
    return jax.shard_map(
        local,
        mesh=fine,
        in_specs=placed,
        out_specs=(P(dp, None, tp), P(dp, tp, None, None)),
        check_vma=False,
    )
```

```python
import functools
import jax
import jax.numpy as jnp
import numpy as np
from jax import lax
from jax.experimental import pallas as pl
from jax.experimental.pallas import tpu as pltpu
from jax.sharding import Mesh, PartitionSpec as P

F32 = jnp.float32
BF16 = jnp.bfloat16
SIZES = {"y": 4, "zl": 2, "c": 2, "x": 4, "zh": 4}
ROWS = 8
HALF = 4
NEW = 64
NT = (((1,), (1,)), ((), ()))
TN = (((0,), (0,)), ((), ()))
LIMIT = pltpu.CompilerParams(vmem_limit_bytes=16 << 20)
WIDE = pltpu.CompilerParams(vmem_limit_bytes=57 << 20)
FREE = pl.CostEstimate(flops=0, bytes_accessed=0, transcendentals=0)
ANYWHERE = pl.BlockSpec(memory_space=pl.ANY)
STATE = (1, 8, 64, 128)

LEAVE, ORDER, LENGTH, CODE, INDEX = 0, 8, 16, 24, 32
BESIDE, BESIDE_ROW, ACROSS, ACROSS_ROW = 40, 48, 56, 64
X_AT, C_AT, ZH_AT = 72, 73, 74


def shift(value, axis, step):
    size = SIZES[axis]
    return lax.ppermute(value, axis, [(i, (i + step) % size) for i in range(size)])


def flip(value, mask):
    return lax.ppermute(value, "x", [(i, i ^ mask) for i in range(4)])


def route_kernel(place, lengths, anchor, out):
    y, zl, c, x, zh = (place[k] for k in range(5))
    me = (y * 2 + zl) * 2 + c
    lane = lax.broadcasted_iota(jnp.int32, (128, 128), 1)
    sub = lax.broadcasted_iota(jnp.int32, (128, 128), 0)
    here = jnp.broadcast_to(anchor[...].astype(F32), (128, 128))
    a_i = here.astype(jnp.int32)
    a_j = jnp.transpose(here).astype(jnp.int32)
    one = lambda mask: jnp.where(mask, 1, 0)
    earlier = one(sub < lane)
    same_dest = one((sub >> 3) == (lane >> 3))
    moves_i = one((a_i >> 3) != (lane >> 3))
    moves_j = one((a_j >> 3) != (sub >> 3))
    total = lambda m: jnp.sum(m.astype(F32), axis=0, keepdims=True).astype(jnp.int32)
    leave_slot = total(moves_j * one((a_j >> 3) == (a_i >> 3)) * earlier)
    before = moves_j * same_dest * earlier
    column_slot = total(before * one(((a_j >> 3) & 3) == ((a_i >> 3) & 3)))
    side_slot = total(before * one(((a_j >> 4) & 1) == ((a_i >> 4) & 1)))
    alike = one(moves_j == moves_i) * earlier
    rank = total(same_dest * (alike + moves_i * (1 - moves_j)))

    row = lambda v: jnp.broadcast_to(v, (8, 128))
    lane8 = lax.broadcasted_iota(jnp.int32, (8, 128), 1)
    q = lax.broadcasted_iota(jnp.int32, (8, 128), 0)
    a8 = row(a_i[0:1])
    leave8, column8, side8, rank8 = row(leave_slot), row(column_slot), row(side_slot), row(rank)
    source = a8 >> 3
    dest = lane8 >> 3
    moving = one(source != dest)
    source_row = a8 & 7
    hops = ((dest >> 2) - (source >> 2)) & 3
    same_zl = one(((source ^ dest) & 2) == 0)
    same_c = one(((source ^ dest) & 1) == 0)
    pick = lambda mask, yes, no: jnp.where(mask == 1, yes, no)
    code = moving * pick(same_zl, pick(same_c, 1 + hops, 5), 6)
    index = pick(
        moving, pick(same_zl, pick(same_c, leave8, column8), side8), source_row
    )
    length8 = jnp.zeros((8, 128), jnp.int32)
    for j in range(ROWS):
        length8 = jnp.where((lane8 & 7) == j, lengths[j], length8)
    take = lambda mask, value: jnp.sum((mask * value).astype(F32), axis=1, keepdims=True)
    leaving = moving * one(source == me) * one(leave8 == q)
    mine = one(dest == me) * one(rank8 == q)
    target = jnp.where(q < 4, (y * 2 + zl) * 2, (y * 2 + 1 - zl) * 2) + 1 - c
    beside = moving * one((source & 3) == zl * 2 + c) * one(dest == target)
    beside = beside * one(column8 == (q & 3))
    across = moving * one(((source >> 1) & 1) == zl) * one(dest == (y * 2 + 1 - zl) * 2 + c)
    across = across * one(side8 == q)
    own_column = one((source & 1) == c)
    parts = [
        take(leaving, source_row),
        take(mine, lane8 & 7),
        take(mine, length8),
        take(mine, code),
        take(mine, index),
        take(beside, hops),
        take(beside, leave8),
        take(across, pick(own_column, hops, 4)),
        take(across, pick(own_column, leave8, 4 + column8)),
    ]
    at = q[:, 0:1]
    tail = jnp.where(at == 0, x, jnp.where(at == 1, c, jnp.where(at == 2, zh, 0))).astype(F32)
    parts.append(tail)
    parts.append(jnp.zeros((128 - 8 * len(parts), 1), F32))
    column = jnp.concatenate(parts, axis=0)
    table = jnp.transpose(jnp.broadcast_to(column, (128, 128)))
    out[...] = table[0:1].astype(jnp.int32)


def route(place, tool_length, anchor):
    smem = pl.BlockSpec(memory_space=pltpu.SMEM)
    table = pl.pallas_call(
        route_kernel,
        in_specs=[smem, smem, pl.BlockSpec(memory_space=pltpu.VMEM)],
        out_specs=pl.BlockSpec(memory_space=pltpu.VMEM),
        out_shape=jax.ShapeDtypeStruct((1, 128), jnp.int32),
        compiler_params=LIMIT,
        cost_estimate=FREE,
        name="route",
    )(place, tool_length, anchor.reshape(1, 128))
    return table.reshape(128)


def per_head(ref):
    first = lax.broadcasted_iota(jnp.int32, (1, 128), 1) < 64
    return jnp.concatenate([jnp.where(first, ref[2 * p], ref[2 * p + 1]) for p in range(4)], axis=0)


def add_kernel(first, second, after, out):
    out[...] = first[...] + second[...]


def add(first, second, after):
    whole = pl.BlockSpec(memory_space=pltpu.VMEM)
    return pl.pallas_call(
        add_kernel,
        in_specs=[whole, whole, ANYWHERE],
        out_specs=whole,
        out_shape=jax.ShapeDtypeStruct(first.shape, F32),
        compiler_params=LIMIT,
        cost_estimate=FREE,
        name="add",
    )(first, second, after)


def trade(value, mask):
    return lax.ppermute(value, "zh", [(i, i ^ mask) for i in range(4)])


def product(left, right):
    return jnp.dot(left, right, preferred_element_type=F32)


def thirds(value):
    parts = []
    for _ in range(3):
        parts.append(value.astype(BF16))
        value = value - parts[-1].astype(F32)
    return parts


def ssm_kernel(start, count, unused, sc, x_ref, g_ref, b_ref, c_ref, dt_ref, bias, rate, skip, *refs):
    sources, refs = refs[:count], refs[count + unused :]
    gated_ref, sq_ref, new_ref, s_all, sems = refs
    r = pl.program_id(0)
    length = sc[LENGTH + start + r]

    @pl.when(r == 0)
    def _():
        for k in range(HALF):
            for which, source in enumerate(sources):

                @pl.when(sc[CODE + start + k] == which)
                def _():
                    pltpu.make_async_copy(
                        source.at[sc[INDEX + start + k]], s_all.at[k], sems.at[k]
                    ).start()

    pltpu.make_async_copy(sources[0].at[0], s_all.at[r], sems.at[r]).wait()
    held = s_all.at[r]
    lane = lax.broadcasted_iota(jnp.int32, (NEW, 128), 1)
    sub = lax.broadcasted_iota(jnp.int32, (NEW, 128), 0)
    within = lane & 63
    causal = within <= sub
    eye = within == sub
    first_half = lane < 64
    live = sub < length
    rows = lax.broadcasted_iota(jnp.int32, (128, 128), 0)
    cols = lax.broadcasted_iota(jnp.int32, (128, 128), 1)
    same = (rows >> 6) == (cols >> 6)
    same_head = jnp.where(same, 1.0, 0.0).astype(BF16)
    upper = jnp.where(same & (rows <= cols), 1.0, 0.0).astype(BF16)
    bias4, rate4, skip4 = per_head(bias), per_head(rate), per_head(skip)
    steps = dt_ref[0]
    raw = bias4 + jnp.concatenate(
        [
            jnp.concatenate([steps[2 * p : 2 * p + 1], steps[2 * p + 1 : 2 * p + 2]], axis=1)
            for p in range(4)
        ],
        axis=0,
    )
    soft = jnp.maximum(raw, 0.0) + jnp.log1p(jnp.exp(-jnp.abs(raw)))
    lane4 = lax.broadcasted_iota(jnp.int32, (4, 128), 1) & 63
    dt4 = jnp.where(lane4 < length, soft, 0.0)
    a4 = -rate4 * dt4
    pieces = [jnp.where(causal, a4[p : p + 1], 0.0) for p in range(4)]
    pieces += [jnp.where(eye, dt4[p : p + 1], 0.0) for p in range(4)]
    spread = sum(product(part, same_head) for part in thirds(jnp.concatenate(pieces, axis=0)))
    stacked = jnp.concatenate([part.astype(F32) for part in thirds(a4)] + [a4 * 0.0], axis=0)
    both = product(stacked.astype(BF16), jnp.concatenate([upper, same_head], axis=1))
    both = both[0:4] + both[4:8] + both[8:12]
    ds4, tot4 = both[:, :128], both[:, 128:]
    wide = lax.broadcasted_iota(jnp.int32, (NEW, 4 * NEW), 1)
    tall = lax.broadcasted_iota(jnp.int32, (NEW, 4 * NEW), 0)
    group = jnp.where(wide == 4 * tall + sc[X_AT], 1.0, 0.0).astype(BF16)
    c_val = jnp.dot(group, c_ref[0], preferred_element_type=F32).astype(BF16)
    b_val = jnp.dot(group, b_ref[0], preferred_element_type=F32).astype(BF16)
    bb = jnp.concatenate([b_val, b_val], axis=0)
    affinity = lax.dot_general(c_val, bb, NT, preferred_element_type=F32)
    affinity = jnp.where(causal, affinity, 0.0)
    squares = jnp.zeros((NEW, 128), F32)
    for p in range(4):
        ds_t = spread[p * NEW : (p + 1) * NEW]
        dt_t = spread[(4 + p) * NEW : (5 + p) * NEW]
        mix = affinity * jnp.exp(ds_t - ds4[p : p + 1]) * dt4[p : p + 1]
        hi = mix.astype(BF16)
        lo = (mix - hi.astype(F32)).astype(BF16)
        xf = x_ref[0, :, p * 128 : (p + 1) * 128].astype(F32)
        blocks = jnp.concatenate(
            [jnp.where(first_half, xf, 0.0), jnp.where(first_half, 0.0, xf)], axis=0
        ).astype(BF16)
        inner = jnp.dot(hi, blocks, preferred_element_type=F32) + jnp.dot(
            lo, blocks, preferred_element_type=F32
        )
        state = held[2 * p : 2 * p + 2].reshape(128, 128)
        carried = lax.dot_general(c_val, state, NT, preferred_element_type=F32)
        out = inner + carried * jnp.exp(ds_t) + skip4[p : p + 1] * xf
        gf = g_ref[0, :, p * 128 : (p + 1) * 128].astype(F32)
        gated = jnp.where(live, out * (gf / (1.0 + jnp.exp(-gf))), 0.0)
        gated_ref[0, :, p * 128 : (p + 1) * 128] = gated
        squares = squares + gated * gated
        weighted = xf * (jnp.exp(tot4[p : p + 1] - ds_t) * dt_t)
        w_hi = weighted.astype(BF16)
        w_lo = (weighted - w_hi.astype(F32)).astype(BF16)
        both = jnp.concatenate([w_hi, w_lo], axis=0)
        update = lax.dot_general(both, bb, TN, preferred_element_type=F32)
        e_tot = jnp.exp(tot4[p : p + 1])
        for k in range(2):
            kept = state[k * 64 : (k + 1) * 64].astype(F32) * e_tot[:, k * 64 : k * 64 + 1]
            new_ref[0, 2 * p + k] = (kept + update[k * 64 : (k + 1) * 64]).astype(BF16)
    ones = jnp.ones((8, 128), BF16)
    sq = sum(
        lax.dot_general(ones, part, NT, preferred_element_type=F32) for part in thirds(squares)[:2]
    )
    sq_ref[0] = sq[0:1]


def run_ssm(table, start, x, gate, b, c, dt, scalars, sources, alias, after=()):
    row3 = lambda r, sc: (sc[ORDER + start + r], 0, 0)
    smem = pl.BlockSpec(memory_space=pltpu.SMEM)
    in_specs = [
        pl.BlockSpec((1, NEW, 512), row3),
        pl.BlockSpec((1, NEW, 512), row3),
        pl.BlockSpec((1, 4 * NEW, 128), row3),
        pl.BlockSpec((1, 4 * NEW, 128), row3),
        pl.BlockSpec((1, 8, NEW), row3),
        *[smem] * 3,
        *[ANYWHERE] * (len(sources) + len(after)),
    ]
    operands = [table, x, gate, b, c, dt, *scalars, *sources, *after]
    unused = len(after)
    aliases = {}
    if alias is not None:
        in_specs.append(ANYWHERE)
        aliases = {len(operands): 2}
        operands.append(alias)
        unused += 1
    return pl.pallas_call(
        functools.partial(ssm_kernel, start, len(sources), unused),
        grid_spec=pltpu.PrefetchScalarGridSpec(
            num_scalar_prefetch=1,
            grid=(HALF,),
            in_specs=in_specs,
            out_specs=[
                pl.BlockSpec((1, NEW, 512), lambda r, sc: (r, 0, 0)),
                pl.BlockSpec((1, 1, NEW), lambda r, sc: (r, 0, 0)),
                pl.BlockSpec(STATE, lambda r, sc: (sc[ORDER + start + r], 0, 0, 0)),
            ],
            scratch_shapes=[
                pltpu.VMEM((HALF, 8, 64, 128), BF16),
                pltpu.SemaphoreType.DMA((HALF,)),
            ],
        ),
        out_shape=[
            jax.ShapeDtypeStruct((HALF, NEW, 512), F32),
            jax.ShapeDtypeStruct((HALF, 1, NEW), F32),
            jax.ShapeDtypeStruct((ROWS, 8, 64, 128), BF16),
        ],
        input_output_aliases=aliases,
        compiler_params=LIMIT,
        cost_estimate=FREE,
        name="ssm",
    )(*operands)


def normalise_kernel(count, gated, *refs):
    sums, (gain, after, out) = refs[:count], refs[count:]
    rows = lax.broadcasted_iota(jnp.int32, (NEW, NEW), 0)
    cols = lax.broadcasted_iota(jnp.int32, (NEW, NEW), 1)
    for r in range(HALF):
        total = sum(part[r] for part in sums)
        scale = lax.rsqrt(total / 2048.0 + 1e-05)
        column = jnp.sum(jnp.where(rows == cols, scale, 0.0), axis=1, keepdims=True)
        out[r * NEW : (r + 1) * NEW] = (gated[r] * column * gain[...]).astype(BF16)


def normalise(gated, sums, gain, after):
    whole = pl.BlockSpec(memory_space=pltpu.VMEM)
    return pl.pallas_call(
        functools.partial(normalise_kernel, len(sums)),
        in_specs=[whole] * (2 + len(sums)) + [ANYWHERE],
        out_specs=whole,
        out_shape=jax.ShapeDtypeStruct((HALF * NEW, 512), BF16),
        compiler_params=LIMIT,
        cost_estimate=FREE,
        name="normalise",
    )(gated, *sums, gain, after)


def project_kernel(sc, a, near0, near1, w0, w1, got, other, after, *outs):
    count = len(outs) // 2
    rows = a.shape[0] // count

    def store(side, value):
        for k in range(count):
            outs[side * count + k][...] = value[k * rows : (k + 1) * rows].astype(BF16)

    for side, near, w in ((0, near0, w0), (1, near1, w1)):

        @pl.when(sc[C_AT] == 1)
        def _():
            store(side, product(a[...], w[...]) + product(near[...], got[side]))

        @pl.when(sc[C_AT] != 1)
        def _():
            store(side, product(a[...], w[...]) + product(near[...], other[side]))


def project(table, a, nears, parts, weights, after, count=1):
    rows = HALF * NEW
    whole = pl.BlockSpec(memory_space=pltpu.VMEM)
    return pl.pallas_call(
        project_kernel,
        grid_spec=pltpu.PrefetchScalarGridSpec(
            num_scalar_prefetch=1,
            grid=(1,),
            in_specs=[whole] * 7 + [ANYWHERE],
            out_specs=[whole] * (2 * count),
        ),
        out_shape=[jax.ShapeDtypeStruct((rows // count, 1024), BF16)] * (2 * count),
        compiler_params=LIMIT,
        cost_estimate=FREE,
        name="project",
    )(table, a, *nears, *parts, *weights, after)


def base_kernel(sc, a, near0, near1, w, got, other, after, out):
    for side, near in ((0, near0), (1, near1)):
        columns = slice(side * 1024, (side + 1) * 1024)

        @pl.when(sc[C_AT] == 0)
        def _():
            out[:, columns] = product(a[...], w[:, columns]) + product(near[...], got[side])

        @pl.when(sc[C_AT] != 0)
        def _():
            out[:, columns] = product(a[...], w[:, columns]) + product(near[...], other[side])


def base_project(table, a, nears, own, weights, after):
    rows = HALF * NEW
    whole = pl.BlockSpec(memory_space=pltpu.VMEM)
    return pl.pallas_call(
        base_kernel,
        grid_spec=pltpu.PrefetchScalarGridSpec(
            num_scalar_prefetch=1,
            grid=(1,),
            in_specs=[whole] * 6 + [ANYWHERE],
            out_specs=whole,
        ),
        out_shape=jax.ShapeDtypeStruct((rows, 2048), F32),
        compiler_params=LIMIT,
        cost_estimate=FREE,
        name="base",
    )(table, a, *nears, own, *weights, after)


def combine_kernel(sc, base, e0, e1, *refs):
    z0, z1, z2, z3 = refs[-4:]
    j = pl.program_id(0)
    arrived = jnp.where((sc[ZH_AT] + j) % 4 < 2, e0[...].astype(F32), e1[...].astype(F32))
    value = base[...] + arrived

    @pl.when(j == 0)
    def _():
        z0[...] = value

    for k, ref in ((1, z1), (2, z2), (3, z3)):

        @pl.when(j == k)
        def _():
            ref[...] = value.astype(BF16)


def combine(table, base, e0, e1, after, part=0):
    rows = e0.shape[0]
    whole = pl.BlockSpec((rows, 512), lambda j, sc: (0, 0))
    at = lambda j, sc: (sc[ZH_AT] + j) % 4
    return pl.pallas_call(
        combine_kernel,
        grid_spec=pltpu.PrefetchScalarGridSpec(
            num_scalar_prefetch=1,
            grid=(4,),
            in_specs=[
                pl.BlockSpec((rows, 512), lambda j, sc: (part, at(j, sc))),
                pl.BlockSpec((rows, 512), lambda j, sc: (0, jnp.minimum(at(j, sc), 1))),
                pl.BlockSpec((rows, 512), lambda j, sc: (0, jnp.maximum(at(j, sc) - 2, 0))),
                *[ANYWHERE] * len(after),
            ],
            out_specs=[whole] * 4,
        ),
        out_shape=[
            jax.ShapeDtypeStruct((rows, 512), F32),
            *[jax.ShapeDtypeStruct((rows, 512), BF16) for _ in range(3)],
        ],
        compiler_params=LIMIT,
        cost_estimate=FREE,
        name="combine",
    )(table, base, e0, e1, *after)


def slice_kernel(first, count, sc, *refs):
    w, outs, sems = refs[0], refs[2 : 2 + count], refs[-1]
    x, c = sc[X_AT], sc[C_AT]
    starts = [(x ^ 1 ^ (3 * c)) * 2, (x ^ 3 ^ c) * 2 + 1, (x ^ 3) * 2, (x ^ 1) * 2 + 1, x]
    copies = []
    for k, out in enumerate(outs):
        start = starts[first + k]
        width = out.shape[1]
        columns = pl.ds(pl.multiple_of(start * width, width), width)
        for part in range(4):
            rows = pl.ds(part * 128, 128)
            copies.append(
                pltpu.make_async_copy(w.at[rows, columns], out.at[rows], sems.at[k, part])
            )
            copies[-1].start()
    for copy in copies:
        copy.wait()


def slices(table, w, after, first, last):
    widths = [1024, 1024, 1024, 1024, 2048][first:last]
    return pl.pallas_call(
        functools.partial(slice_kernel, first, len(widths)),
        grid_spec=pltpu.PrefetchScalarGridSpec(
            num_scalar_prefetch=1,
            grid=(1,),
            in_specs=[ANYWHERE] * 2,
            out_specs=[pl.BlockSpec(memory_space=pltpu.VMEM)] * len(widths),
            scratch_shapes=[pltpu.SemaphoreType.DMA((len(widths), 4))],
        ),
        out_shape=[jax.ShapeDtypeStruct((512, width), BF16) for width in widths],
        compiler_params=WIDE if first == 0 else LIMIT,
        cost_estimate=FREE,
        name="slices",
    )(table, w, after)


def wait_kernel(after, out):
    out[...] = jnp.zeros_like(out)


def wait(after):
    return pl.pallas_call(
        wait_kernel,
        in_specs=[ANYWHERE],
        out_specs=pl.BlockSpec(memory_space=pltpu.VMEM),
        out_shape=jax.ShapeDtypeStruct((8, 128), F32),
        compiler_params=LIMIT,
        cost_estimate=pl.CostEstimate(flops=0, bytes_accessed=16 << 20, transcendentals=0),
        name="wait",
    )(after)


def hold_kernel(value, after, out):
    pass


def hold(value, after):
    return pl.pallas_call(
        hold_kernel,
        in_specs=[ANYWHERE] * 2,
        out_specs=ANYWHERE,
        out_shape=jax.ShapeDtypeStruct(value.shape, value.dtype),
        input_output_aliases={0: 0},
        compiler_params=LIMIT,
        cost_estimate=FREE,
        name="hold",
    )(value, after)


def join_kernel(first, second, after, out, sems):
    copies = [
        pltpu.make_async_copy(ref, out.at[k], sems.at[k]) for k, ref in enumerate((first, second))
    ]
    for copy in copies:
        copy.start()
    for copy in copies:
        copy.wait()


def join(first, second, after):
    return pl.pallas_call(
        join_kernel,
        in_specs=[ANYWHERE] * 3,
        out_specs=pl.BlockSpec(memory_space=pltpu.VMEM),
        out_shape=jax.ShapeDtypeStruct((2, *first.shape), first.dtype),
        scratch_shapes=[pltpu.SemaphoreType.DMA((2,))],
        compiler_params=LIMIT,
        cost_estimate=FREE,
        name="join",
    )(first, second, after)


def gather_kernel(*refs):
    out = refs[-1]
    value = refs[0][...]
    for part in refs[1:-1]:
        value = value + part[...].astype(F32)
    out[...] = value.astype(out.dtype)


def gather_sum(parts, dtype):
    whole = pl.BlockSpec(memory_space=pltpu.VMEM)
    return pl.pallas_call(
        gather_kernel,
        in_specs=[whole] * len(parts),
        out_specs=whole,
        out_shape=jax.ShapeDtypeStruct(parts[0].shape, dtype),
        compiler_params=LIMIT,
        cost_estimate=FREE,
        name="gather_sum",
    )(*parts)


def finish_kernel(sc, half, *refs):
    parts, (out, held, sem) = refs[:-3], refs[-3:]

    def rows_out(source, p):
        rows = pl.ds(p % HALF * NEW, NEW)
        return pltpu.make_async_copy(source.at[rows], out.at[sc[ORDER + p]], sem.at[p])

    copies = [rows_out(half, p) for p in range(HALF)]
    copies += [rows_out(held, p) for p in range(HALF, ROWS)]
    for p in range(HALF):
        copies[p].start()
    at = 0
    for count in 2, 4:
        group, parts = parts[:count], parts[count:]
        value = group[0][...]
        for part in group[1:]:
            value = value + part[...].astype(F32)
        held[at : at + value.shape[0]] = value.astype(BF16)
        at += value.shape[0]
    for p in range(HALF, ROWS):
        copies[p].start()
    for copy in copies:
        copy.wait()


def finish(table, half, parts):
    whole = pl.BlockSpec(memory_space=pltpu.VMEM)
    return pl.pallas_call(
        finish_kernel,
        grid_spec=pltpu.PrefetchScalarGridSpec(
            num_scalar_prefetch=1,
            grid=(1,),
            in_specs=[whole] * (1 + len(parts)),
            out_specs=ANYWHERE,
            scratch_shapes=[
                pltpu.VMEM((HALF * NEW, 512), BF16),
                pltpu.SemaphoreType.DMA((ROWS,)),
            ],
        ),
        out_shape=jax.ShapeDtypeStruct((ROWS, NEW, 512), BF16),
        compiler_params=LIMIT,
        cost_estimate=FREE,
        name="finish",
    )(table, half, *parts)


def copy_kernel(sc, source, out):
    out[...] = source[...]


def leave(table, states):
    return pl.pallas_call(
        copy_kernel,
        grid_spec=pltpu.PrefetchScalarGridSpec(
            num_scalar_prefetch=1,
            grid=(HALF,),
            in_specs=[pl.BlockSpec(STATE, lambda q, sc: (sc[LEAVE + q], 0, 0, 0))],
            out_specs=pl.BlockSpec(STATE, lambda q, sc: (q, 0, 0, 0)),
        ),
        out_shape=jax.ShapeDtypeStruct((HALF, 8, 64, 128), BF16),
        compiler_params=LIMIT,
        cost_estimate=FREE,
        name="leave",
    )(table, states)


def pick_kernel(count, start, start_row, sc, *refs):
    sources, out, sems = refs[:count], refs[-2], refs[-1]
    slots = out.shape[0]
    for q in range(slots):
        for which in range(count):

            @pl.when(sc[start + q] == which)
            def _():
                row = sc[start_row + q]
                pltpu.make_async_copy(sources[which].at[row], out.at[q], sems.at[q]).start()

    for q in range(slots):
        pltpu.make_async_copy(sources[0].at[0], out.at[q], sems.at[q]).wait()


def pick(table, sources, start, start_row, slots, after):
    return pl.pallas_call(
        functools.partial(pick_kernel, len(sources), start, start_row),
        grid_spec=pltpu.PrefetchScalarGridSpec(
            num_scalar_prefetch=1,
            grid=(1,),
            in_specs=[ANYWHERE] * (len(sources) + 1),
            out_specs=pl.BlockSpec(memory_space=pltpu.VMEM),
            scratch_shapes=[pltpu.SemaphoreType.DMA((slots,))],
        ),
        out_shape=jax.ShapeDtypeStruct((slots, 8, 64, 128), BF16),
        compiler_params=LIMIT,
        cost_estimate=FREE,
        name="pick",
    )(table, *sources, after)


def local(
    ssm_input,
    gate_input,
    write_basis,
    read_basis,
    step_raw,
    step_bias,
    decay_rate,
    skip_gain,
    norm_gain,
    out_weight,
    ssm_states,
    anchor,
    tool_length,
):
    place = jnp.stack([lax.axis_index(n) for n in ("y", "zl", "c", "x", "zh")]).astype(jnp.int32)
    table = route(place, tool_length, anchor)
    buf = leave(table, ssm_states)
    along = [buf] + [shift(buf, "y", k) for k in (1, 2, 3)]

    shares = slices(table, out_weight, buf, 0, 2)
    got = [flip(shares[0], 1), flip(shares[1], 3)]

    b = write_basis.reshape(ROWS, 4 * NEW, 128)
    c = read_basis.reshape(ROWS, 4 * NEW, 128)
    gain = norm_gain.reshape(1, 512)
    ssm = functools.partial(
        run_ssm,
        table,
        x=ssm_input,
        gate=gate_input,
        b=b,
        c=c,
        dt=step_raw,
        scalars=(step_bias, decay_rate, skip_gain),
    )

    def spread_rows(gated, sums, after):
        a = normalise(gated, sums, gain, after)
        return a, [flip(a, 1), flip(a, 3)]

    def reduce_rest(base, moved, after, part=0):
        zs = combine(table, base, *moved, after, part)
        return [zs[0]] + [shift(zs[k], "zh", k) for k in (1, 2, 3)]

    gated1, sq1, states1 = ssm(start=0, sources=[ssm_states], alias=None, after=[shares[0]])
    sums1 = lax.psum(sq1, "zh")

    chosen = pick(table, along, BESIDE, BESIDE_ROW, 8, sums1)
    beside = shift(chosen, "c", 1)
    near_weights = join(*got, wait(chosen))
    a1, nears1 = spread_rows(gated1, [sums1], near_weights)
    picked = pick(table, [*along, beside], ACROSS, ACROSS_ROW, HALF, a1)
    across = shift(picked, "zl", 1)
    near_weights = hold(near_weights, picked)
    weights = [near_weights, shift(near_weights, "c", 1)]
    part0, part1, own = slices(table, out_weight, picked, 2, 5)
    sent1 = project(table, a1, nears1, [part0, part1], weights, picked)
    moved1 = [flip(sent1[0], 3), flip(sent1[1], 1)]
    base1 = base_project(table, a1, nears1, own, weights, sent1[0])

    gated2, sq2, new_states = ssm(
        start=HALF, sources=[ssm_states, *along, beside, across], alias=states1, after=[base1]
    )
    near_sums = trade(sq2, 1)
    z0, r1, r2, r3 = reduce_rest(base1, moved1, [sq2])
    half_sums = add(sq2, near_sums, z0)
    a2, nears2 = spread_rows(gated2, [half_sums, trade(half_sums, 3)], z0)
    gathered = gather_sum([z0, r1, r3], F32)
    sent2 = project(table, a2, nears2, [part0, part1], weights, gathered, 2)
    moved2 = [[flip(sent2[k], 3), flip(sent2[2 + k], 1)] for k in range(2)]
    base2 = base_project(table, a2, nears2, own, weights, sent2[0])
    z0, r1, late, r3 = reduce_rest(base2, moved2[0], [base2], 0)
    gathered2 = gather_sum([z0, r1, r3], F32)
    half_out = gather_sum([gathered, r2], BF16)
    done2 = reduce_rest(base2, moved2[1], [half_out, gathered2], 1)
    return finish(table, half_out, [gathered2, late, *done2]), new_states


def solution(mesh):
    fine = Mesh(mesh.devices.reshape(4, 2, 2, 4, 4), ("y", "zl", "c", "x", "zh"))
    dp, tp = ("y", "zl", "c"), ("x", "zh")
    placed = (
        P(dp, None, tp),
        P(dp, None, tp),
        P(dp, None, None, None),
        P(dp, None, None, None),
        P(dp, tp, None),
        P(tp),
        P(tp),
        P(tp),
        P(tp),
        P(tp, None),
        P(dp, tp, None, None),
        P(),
        P(dp),
    )
    return jax.shard_map(
        local,
        mesh=fine,
        in_specs=placed,
        out_specs=(P(dp, None, tp), P(dp, tp, None, None)),
        check_vma=False,
    )
```

```python
import functools
import jax
import jax.numpy as jnp
import numpy as np
from jax import lax
from jax.experimental import pallas as pl
from jax.experimental.pallas import tpu as pltpu
from jax.sharding import Mesh, PartitionSpec as P

F32 = jnp.float32
BF16 = jnp.bfloat16
SIZES = {"y": 4, "zl": 2, "c": 2, "x": 4, "zh": 4}
ROWS = 8
HALF = 4
NEW = 64
NT = (((1,), (1,)), ((), ()))
TN = (((0,), (0,)), ((), ()))
LIMIT = pltpu.CompilerParams(vmem_limit_bytes=16 << 20)
WIDE = pltpu.CompilerParams(vmem_limit_bytes=57 << 20)
FREE = pl.CostEstimate(flops=0, bytes_accessed=0, transcendentals=0)
ANYWHERE = pl.BlockSpec(memory_space=pl.ANY)
STATE = (1, 8, 64, 128)

LEAVE, ORDER, LENGTH, CODE, INDEX = 0, 8, 16, 24, 32
BESIDE, BESIDE_ROW, ACROSS, ACROSS_ROW = 40, 48, 56, 64
X_AT, C_AT, ZH_AT = 72, 73, 74


def shift(value, axis, step):
    size = SIZES[axis]
    return lax.ppermute(value, axis, [(i, (i + step) % size) for i in range(size)])


def flip(value, mask):
    return lax.ppermute(value, "x", [(i, i ^ mask) for i in range(4)])


def route_kernel(place, lengths, anchor, out):
    y, zl, c, x, zh = (place[k] for k in range(5))
    me = (y * 2 + zl) * 2 + c
    lane = lax.broadcasted_iota(jnp.int32, (128, 128), 1)
    sub = lax.broadcasted_iota(jnp.int32, (128, 128), 0)
    here = jnp.broadcast_to(anchor[...].astype(F32), (128, 128))
    a_i = here.astype(jnp.int32)
    a_j = jnp.transpose(here).astype(jnp.int32)
    one = lambda mask: jnp.where(mask, 1, 0)
    earlier = one(sub < lane)
    same_dest = one((sub >> 3) == (lane >> 3))
    moves_i = one((a_i >> 3) != (lane >> 3))
    moves_j = one((a_j >> 3) != (sub >> 3))
    total = lambda m: jnp.sum(m.astype(F32), axis=0, keepdims=True).astype(jnp.int32)
    leave_slot = total(moves_j * one((a_j >> 3) == (a_i >> 3)) * earlier)
    before = moves_j * same_dest * earlier
    column_slot = total(before * one(((a_j >> 3) & 3) == ((a_i >> 3) & 3)))
    side_slot = total(before * one(((a_j >> 4) & 1) == ((a_i >> 4) & 1)))
    alike = one(moves_j == moves_i) * earlier
    rank = total(same_dest * (alike + moves_i * (1 - moves_j)))

    row = lambda v: jnp.broadcast_to(v, (8, 128))
    lane8 = lax.broadcasted_iota(jnp.int32, (8, 128), 1)
    q = lax.broadcasted_iota(jnp.int32, (8, 128), 0)
    a8 = row(a_i[0:1])
    leave8, column8, side8, rank8 = row(leave_slot), row(column_slot), row(side_slot), row(rank)
    source = a8 >> 3
    dest = lane8 >> 3
    moving = one(source != dest)
    source_row = a8 & 7
    hops = ((dest >> 2) - (source >> 2)) & 3
    same_zl = one(((source ^ dest) & 2) == 0)
    same_c = one(((source ^ dest) & 1) == 0)
    pick = lambda mask, yes, no: jnp.where(mask == 1, yes, no)
    code = moving * pick(same_zl, pick(same_c, 1 + hops, 5), 6)
    index = pick(
        moving, pick(same_zl, pick(same_c, leave8, column8), side8), source_row
    )
    length8 = jnp.zeros((8, 128), jnp.int32)
    for j in range(ROWS):
        length8 = jnp.where((lane8 & 7) == j, lengths[j], length8)
    take = lambda mask, value: jnp.sum((mask * value).astype(F32), axis=1, keepdims=True)
    leaving = moving * one(source == me) * one(leave8 == q)
    mine = one(dest == me) * one(rank8 == q)
    target = jnp.where(q < 4, (y * 2 + zl) * 2, (y * 2 + 1 - zl) * 2) + 1 - c
    beside = moving * one((source & 3) == zl * 2 + c) * one(dest == target)
    beside = beside * one(column8 == (q & 3))
    across = moving * one(((source >> 1) & 1) == zl) * one(dest == (y * 2 + 1 - zl) * 2 + c)
    across = across * one(side8 == q)
    own_column = one((source & 1) == c)
    parts = [
        take(leaving, source_row),
        take(mine, lane8 & 7),
        take(mine, length8),
        take(mine, code),
        take(mine, index),
        take(beside, hops),
        take(beside, leave8),
        take(across, pick(own_column, hops, 4)),
        take(across, pick(own_column, leave8, 4 + column8)),
    ]
    at = q[:, 0:1]
    tail = jnp.where(at == 0, x, jnp.where(at == 1, c, jnp.where(at == 2, zh, 0))).astype(F32)
    parts.append(tail)
    parts.append(jnp.zeros((128 - 8 * len(parts), 1), F32))
    column = jnp.concatenate(parts, axis=0)
    table = jnp.transpose(jnp.broadcast_to(column, (128, 128)))
    out[...] = table[0:1].astype(jnp.int32)


def route(place, tool_length, anchor):
    smem = pl.BlockSpec(memory_space=pltpu.SMEM)
    table = pl.pallas_call(
        route_kernel,
        in_specs=[smem, smem, pl.BlockSpec(memory_space=pltpu.VMEM)],
        out_specs=pl.BlockSpec(memory_space=pltpu.VMEM),
        out_shape=jax.ShapeDtypeStruct((1, 128), jnp.int32),
        compiler_params=LIMIT,
        cost_estimate=FREE,
        name="route",
    )(place, tool_length, anchor.reshape(1, 128))
    return table.reshape(128)


def per_head(ref):
    first = lax.broadcasted_iota(jnp.int32, (1, 128), 1) < 64
    return jnp.concatenate([jnp.where(first, ref[2 * p], ref[2 * p + 1]) for p in range(4)], axis=0)


def add_kernel(first, second, after, out):
    out[...] = first[...] + second[...]


def add(first, second, after):
    whole = pl.BlockSpec(memory_space=pltpu.VMEM)
    return pl.pallas_call(
        add_kernel,
        in_specs=[whole, whole, ANYWHERE],
        out_specs=whole,
        out_shape=jax.ShapeDtypeStruct(first.shape, F32),
        compiler_params=LIMIT,
        cost_estimate=FREE,
        name="add",
    )(first, second, after)


def trade(value, mask):
    return lax.ppermute(value, "zh", [(i, i ^ mask) for i in range(4)])


def product(left, right):
    return jnp.dot(left, right, preferred_element_type=F32)


def thirds(value):
    parts = []
    for _ in range(3):
        parts.append(value.astype(BF16))
        value = value - parts[-1].astype(F32)
    return parts


def ssm_kernel(start, count, unused, sc, x_ref, g_ref, b_ref, c_ref, dt_ref, bias, rate, skip, *refs):
    sources, refs = refs[:count], refs[count + unused :]
    gated_ref, sq_ref, new_ref, s_all, sems = refs
    r = pl.program_id(0)
    length = sc[LENGTH + start + r]

    @pl.when(r == 0)
    def _():
        for k in range(HALF):
            for which, source in enumerate(sources):

                @pl.when(sc[CODE + start + k] == which)
                def _():
                    pltpu.make_async_copy(
                        source.at[sc[INDEX + start + k]], s_all.at[k], sems.at[k]
                    ).start()

    pltpu.make_async_copy(sources[0].at[0], s_all.at[r], sems.at[r]).wait()
    held = s_all.at[r]
    lane = lax.broadcasted_iota(jnp.int32, (NEW, 128), 1)
    sub = lax.broadcasted_iota(jnp.int32, (NEW, 128), 0)
    within = lane & 63
    causal = within <= sub
    eye = within == sub
    first_half = lane < 64
    live = sub < length
    rows = lax.broadcasted_iota(jnp.int32, (128, 128), 0)
    cols = lax.broadcasted_iota(jnp.int32, (128, 128), 1)
    same = (rows >> 6) == (cols >> 6)
    same_head = jnp.where(same, 1.0, 0.0).astype(BF16)
    upper = jnp.where(same & (rows <= cols), 1.0, 0.0).astype(BF16)
    bias4, rate4, skip4 = per_head(bias), per_head(rate), per_head(skip)
    steps = dt_ref[0]
    raw = bias4 + jnp.concatenate(
        [
            jnp.concatenate([steps[2 * p : 2 * p + 1], steps[2 * p + 1 : 2 * p + 2]], axis=1)
            for p in range(4)
        ],
        axis=0,
    )
    soft = jnp.maximum(raw, 0.0) + jnp.log1p(jnp.exp(-jnp.abs(raw)))
    lane4 = lax.broadcasted_iota(jnp.int32, (4, 128), 1) & 63
    dt4 = jnp.where(lane4 < length, soft, 0.0)
    a4 = -rate4 * dt4
    pieces = [jnp.where(causal, a4[p : p + 1], 0.0) for p in range(4)]
    pieces += [jnp.where(eye, dt4[p : p + 1], 0.0) for p in range(4)]
    spread = sum(product(part, same_head) for part in thirds(jnp.concatenate(pieces, axis=0)))
    stacked = jnp.concatenate([part.astype(F32) for part in thirds(a4)] + [a4 * 0.0], axis=0)
    both = product(stacked.astype(BF16), jnp.concatenate([upper, same_head], axis=1))
    both = both[0:4] + both[4:8] + both[8:12]
    ds4, tot4 = both[:, :128], both[:, 128:]
    wide = lax.broadcasted_iota(jnp.int32, (NEW, 4 * NEW), 1)
    tall = lax.broadcasted_iota(jnp.int32, (NEW, 4 * NEW), 0)
    group = jnp.where(wide == 4 * tall + sc[X_AT], 1.0, 0.0).astype(BF16)
    c_val = jnp.dot(group, c_ref[0], preferred_element_type=F32).astype(BF16)
    b_val = jnp.dot(group, b_ref[0], preferred_element_type=F32).astype(BF16)
    bb = jnp.concatenate([b_val, b_val], axis=0)
    affinity = lax.dot_general(c_val, bb, NT, preferred_element_type=F32)
    affinity = jnp.where(causal, affinity, 0.0)
    squares = jnp.zeros((NEW, 128), F32)
    for p in range(4):
        ds_t = spread[p * NEW : (p + 1) * NEW]
        dt_t = spread[(4 + p) * NEW : (5 + p) * NEW]
        mix = affinity * jnp.exp(ds_t - ds4[p : p + 1]) * dt4[p : p + 1]
        hi = mix.astype(BF16)
        lo = (mix - hi.astype(F32)).astype(BF16)
        xf = x_ref[0, :, p * 128 : (p + 1) * 128].astype(F32)
        blocks = jnp.concatenate(
            [jnp.where(first_half, xf, 0.0), jnp.where(first_half, 0.0, xf)], axis=0
        ).astype(BF16)
        inner = jnp.dot(hi, blocks, preferred_element_type=F32) + jnp.dot(
            lo, blocks, preferred_element_type=F32
        )
        state = held[2 * p : 2 * p + 2].reshape(128, 128)
        carried = lax.dot_general(c_val, state, NT, preferred_element_type=F32)
        out = inner + carried * jnp.exp(ds_t) + skip4[p : p + 1] * xf
        gf = g_ref[0, :, p * 128 : (p + 1) * 128].astype(F32)
        gated = jnp.where(live, out * (gf / (1.0 + jnp.exp(-gf))), 0.0)
        gated_ref[0, :, p * 128 : (p + 1) * 128] = gated
        squares = squares + gated * gated
        weighted = xf * (jnp.exp(tot4[p : p + 1] - ds_t) * dt_t)
        w_hi = weighted.astype(BF16)
        w_lo = (weighted - w_hi.astype(F32)).astype(BF16)
        both = jnp.concatenate([w_hi, w_lo], axis=0)
        update = lax.dot_general(both, bb, TN, preferred_element_type=F32)
        e_tot = jnp.exp(tot4[p : p + 1])
        for k in range(2):
            kept = state[k * 64 : (k + 1) * 64].astype(F32) * e_tot[:, k * 64 : k * 64 + 1]
            new_ref[0, 2 * p + k] = (kept + update[k * 64 : (k + 1) * 64]).astype(BF16)
    ones = jnp.ones((8, 128), BF16)
    sq = sum(
        lax.dot_general(ones, part, NT, preferred_element_type=F32) for part in thirds(squares)[:2]
    )
    sq_ref[0] = sq[0:1]


def run_ssm(table, start, x, gate, b, c, dt, scalars, sources, alias, after=()):
    row3 = lambda r, sc: (sc[ORDER + start + r], 0, 0)
    smem = pl.BlockSpec(memory_space=pltpu.SMEM)
    in_specs = [
        pl.BlockSpec((1, NEW, 512), row3),
        pl.BlockSpec((1, NEW, 512), row3),
        pl.BlockSpec((1, 4 * NEW, 128), row3),
        pl.BlockSpec((1, 4 * NEW, 128), row3),
        pl.BlockSpec((1, 8, NEW), row3),
        *[smem] * 3,
        *[ANYWHERE] * (len(sources) + len(after)),
    ]
    operands = [table, x, gate, b, c, dt, *scalars, *sources, *after]
    unused = len(after)
    aliases = {}
    if alias is not None:
        in_specs.append(ANYWHERE)
        aliases = {len(operands): 2}
        operands.append(alias)
        unused += 1
    return pl.pallas_call(
        functools.partial(ssm_kernel, start, len(sources), unused),
        grid_spec=pltpu.PrefetchScalarGridSpec(
            num_scalar_prefetch=1,
            grid=(HALF,),
            in_specs=in_specs,
            out_specs=[
                pl.BlockSpec((1, NEW, 512), lambda r, sc: (r, 0, 0)),
                pl.BlockSpec((1, 1, NEW), lambda r, sc: (r, 0, 0)),
                pl.BlockSpec(STATE, lambda r, sc: (sc[ORDER + start + r], 0, 0, 0)),
            ],
            scratch_shapes=[
                pltpu.VMEM((HALF, 8, 64, 128), BF16),
                pltpu.SemaphoreType.DMA((HALF,)),
            ],
        ),
        out_shape=[
            jax.ShapeDtypeStruct((HALF, NEW, 512), F32),
            jax.ShapeDtypeStruct((HALF, 1, NEW), F32),
            jax.ShapeDtypeStruct((ROWS, 8, 64, 128), BF16),
        ],
        input_output_aliases=aliases,
        compiler_params=LIMIT,
        cost_estimate=FREE,
        name="ssm",
    )(*operands)


def normalise_kernel(count, gated, *refs):
    sums, (gain, after, out) = refs[:count], refs[count:]
    rows = lax.broadcasted_iota(jnp.int32, (NEW, NEW), 0)
    cols = lax.broadcasted_iota(jnp.int32, (NEW, NEW), 1)
    for r in range(HALF):
        total = sum(part[r] for part in sums)
        scale = lax.rsqrt(total / 2048.0 + 1e-05)
        column = jnp.sum(jnp.where(rows == cols, scale, 0.0), axis=1, keepdims=True)
        out[r * NEW : (r + 1) * NEW] = (gated[r] * column * gain[...]).astype(BF16)


def normalise(gated, sums, gain, after):
    whole = pl.BlockSpec(memory_space=pltpu.VMEM)
    return pl.pallas_call(
        functools.partial(normalise_kernel, len(sums)),
        in_specs=[whole] * (2 + len(sums)) + [ANYWHERE],
        out_specs=whole,
        out_shape=jax.ShapeDtypeStruct((HALF * NEW, 512), BF16),
        compiler_params=LIMIT,
        cost_estimate=FREE,
        name="normalise",
    )(gated, *sums, gain, after)


def project_kernel(sc, a, near0, near1, w0, w1, got, other, after, *outs):
    count = len(outs) // 2
    rows = a.shape[0] // count

    def store(side, value):
        for k in range(count):
            outs[side * count + k][...] = value[k * rows : (k + 1) * rows].astype(BF16)

    for side, near, w in ((0, near0, w0), (1, near1, w1)):

        @pl.when(sc[C_AT] == 1)
        def _():
            store(side, product(a[...], w[...]) + product(near[...], got[side]))

        @pl.when(sc[C_AT] != 1)
        def _():
            store(side, product(a[...], w[...]) + product(near[...], other[side]))


def project(table, a, nears, parts, weights, after, count=1):
    rows = HALF * NEW
    whole = pl.BlockSpec(memory_space=pltpu.VMEM)
    return pl.pallas_call(
        project_kernel,
        grid_spec=pltpu.PrefetchScalarGridSpec(
            num_scalar_prefetch=1,
            grid=(1,),
            in_specs=[whole] * 7 + [ANYWHERE],
            out_specs=[whole] * (2 * count),
        ),
        out_shape=[jax.ShapeDtypeStruct((rows // count, 1024), BF16)] * (2 * count),
        compiler_params=LIMIT,
        cost_estimate=FREE,
        name="project",
    )(table, a, *nears, *parts, *weights, after)


def base_kernel(sc, a, near0, near1, w, got, other, after, out):
    for side, near in ((0, near0), (1, near1)):
        columns = slice(side * 1024, (side + 1) * 1024)

        @pl.when(sc[C_AT] == 0)
        def _():
            out[:, columns] = product(a[...], w[:, columns]) + product(near[...], got[side])

        @pl.when(sc[C_AT] != 0)
        def _():
            out[:, columns] = product(a[...], w[:, columns]) + product(near[...], other[side])


def base_project(table, a, nears, own, weights, after):
    rows = HALF * NEW
    whole = pl.BlockSpec(memory_space=pltpu.VMEM)
    return pl.pallas_call(
        base_kernel,
        grid_spec=pltpu.PrefetchScalarGridSpec(
            num_scalar_prefetch=1,
            grid=(1,),
            in_specs=[whole] * 6 + [ANYWHERE],
            out_specs=whole,
        ),
        out_shape=jax.ShapeDtypeStruct((rows, 2048), F32),
        compiler_params=LIMIT,
        cost_estimate=FREE,
        name="base",
    )(table, a, *nears, own, *weights, after)


def combine_kernel(sc, base, e0, e1, *refs):
    z0, z1, z2, z3 = refs[-4:]
    j = pl.program_id(0)
    arrived = jnp.where((sc[ZH_AT] + j) % 4 < 2, e0[...].astype(F32), e1[...].astype(F32))
    value = base[...] + arrived

    @pl.when(j == 0)
    def _():
        z0[...] = value

    for k, ref in ((1, z1), (2, z2), (3, z3)):

        @pl.when(j == k)
        def _():
            ref[...] = value.astype(BF16)


def combine(table, base, e0, e1, after, part=0):
    rows = e0.shape[0]
    whole = pl.BlockSpec((rows, 512), lambda j, sc: (0, 0))
    at = lambda j, sc: (sc[ZH_AT] + j) % 4
    return pl.pallas_call(
        combine_kernel,
        grid_spec=pltpu.PrefetchScalarGridSpec(
            num_scalar_prefetch=1,
            grid=(4,),
            in_specs=[
                pl.BlockSpec((rows, 512), lambda j, sc: (part, at(j, sc))),
                pl.BlockSpec((rows, 512), lambda j, sc: (0, jnp.minimum(at(j, sc), 1))),
                pl.BlockSpec((rows, 512), lambda j, sc: (0, jnp.maximum(at(j, sc) - 2, 0))),
                *[ANYWHERE] * len(after),
            ],
            out_specs=[whole] * 4,
        ),
        out_shape=[
            jax.ShapeDtypeStruct((rows, 512), F32),
            *[jax.ShapeDtypeStruct((rows, 512), BF16) for _ in range(3)],
        ],
        compiler_params=LIMIT,
        cost_estimate=FREE,
        name="combine",
    )(table, base, e0, e1, *after)


def slice_kernel(first, count, sc, *refs):
    w, outs, sems = refs[0], refs[2 : 2 + count], refs[-1]
    x, c = sc[X_AT], sc[C_AT]
    starts = [(x ^ 1 ^ (3 * c)) * 2, (x ^ 3 ^ c) * 2 + 1, (x ^ 3) * 2, (x ^ 1) * 2 + 1, x]
    copies = []
    for k, out in enumerate(outs):
        start = starts[first + k]
        width = out.shape[1]
        columns = pl.ds(pl.multiple_of(start * width, width), width)
        for part in range(4):
            rows = pl.ds(part * 128, 128)
            copies.append(
                pltpu.make_async_copy(w.at[rows, columns], out.at[rows], sems.at[k, part])
            )
            copies[-1].start()
    for copy in copies:
        copy.wait()


def slices(table, w, after, first, last):
    widths = [1024, 1024, 1024, 1024, 2048][first:last]
    return pl.pallas_call(
        functools.partial(slice_kernel, first, len(widths)),
        grid_spec=pltpu.PrefetchScalarGridSpec(
            num_scalar_prefetch=1,
            grid=(1,),
            in_specs=[ANYWHERE] * 2,
            out_specs=[pl.BlockSpec(memory_space=pltpu.VMEM)] * len(widths),
            scratch_shapes=[pltpu.SemaphoreType.DMA((len(widths), 4))],
        ),
        out_shape=[jax.ShapeDtypeStruct((512, width), BF16) for width in widths],
        compiler_params=WIDE if first == 0 else LIMIT,
        cost_estimate=FREE,
        name="slices",
    )(table, w, after)


def wait_kernel(after, out):
    out[...] = jnp.zeros_like(out)


def wait(after):
    return pl.pallas_call(
        wait_kernel,
        in_specs=[ANYWHERE],
        out_specs=pl.BlockSpec(memory_space=pltpu.VMEM),
        out_shape=jax.ShapeDtypeStruct((8, 128), F32),
        compiler_params=LIMIT,
        cost_estimate=pl.CostEstimate(flops=0, bytes_accessed=16 << 20, transcendentals=0),
        name="wait",
    )(after)


def hold_kernel(value, after, out):
    pass


def hold(value, after):
    return pl.pallas_call(
        hold_kernel,
        in_specs=[ANYWHERE] * 2,
        out_specs=ANYWHERE,
        out_shape=jax.ShapeDtypeStruct(value.shape, value.dtype),
        input_output_aliases={0: 0},
        compiler_params=LIMIT,
        cost_estimate=FREE,
        name="hold",
    )(value, after)


def join_kernel(first, second, after, out, sems):
    copies = [
        pltpu.make_async_copy(ref, out.at[k], sems.at[k]) for k, ref in enumerate((first, second))
    ]
    for copy in copies:
        copy.start()
    for copy in copies:
        copy.wait()


def join(first, second, after):
    return pl.pallas_call(
        join_kernel,
        in_specs=[ANYWHERE] * 3,
        out_specs=pl.BlockSpec(memory_space=pltpu.VMEM),
        out_shape=jax.ShapeDtypeStruct((2, *first.shape), first.dtype),
        scratch_shapes=[pltpu.SemaphoreType.DMA((2,))],
        compiler_params=LIMIT,
        cost_estimate=FREE,
        name="join",
    )(first, second, after)


def gather_kernel(*refs):
    out = refs[-1]
    value = refs[0][...]
    for part in refs[1:-1]:
        value = value + part[...].astype(F32)
    out[...] = value.astype(out.dtype)


def gather_sum(parts, dtype):
    whole = pl.BlockSpec(memory_space=pltpu.VMEM)
    return pl.pallas_call(
        gather_kernel,
        in_specs=[whole] * len(parts),
        out_specs=whole,
        out_shape=jax.ShapeDtypeStruct(parts[0].shape, dtype),
        compiler_params=LIMIT,
        cost_estimate=FREE,
        name="gather_sum",
    )(*parts)


def finish_kernel(sc, half, *refs):
    parts, (out, held, sem) = refs[:-3], refs[-3:]

    def rows_out(source, p):
        rows = pl.ds(p % HALF * NEW, NEW)
        return pltpu.make_async_copy(source.at[rows], out.at[sc[ORDER + p]], sem.at[p])

    copies = [rows_out(half, p) for p in range(HALF)]
    copies += [rows_out(held, p) for p in range(HALF, ROWS)]
    for p in range(HALF):
        copies[p].start()
    at = 0
    for count in 2, 4:
        group, parts = parts[:count], parts[count:]
        value = group[0][...]
        for part in group[1:]:
            value = value + part[...].astype(F32)
        held[at : at + value.shape[0]] = value.astype(BF16)
        at += value.shape[0]
    for p in range(HALF, ROWS):
        copies[p].start()
    for copy in copies:
        copy.wait()


def finish(table, half, parts):
    whole = pl.BlockSpec(memory_space=pltpu.VMEM)
    return pl.pallas_call(
        finish_kernel,
        grid_spec=pltpu.PrefetchScalarGridSpec(
            num_scalar_prefetch=1,
            grid=(1,),
            in_specs=[whole] * (1 + len(parts)),
            out_specs=ANYWHERE,
            scratch_shapes=[
                pltpu.VMEM((HALF * NEW, 512), BF16),
                pltpu.SemaphoreType.DMA((ROWS,)),
            ],
        ),
        out_shape=jax.ShapeDtypeStruct((ROWS, NEW, 512), BF16),
        compiler_params=LIMIT,
        cost_estimate=FREE,
        name="finish",
    )(table, half, *parts)


def copy_kernel(sc, source, out):
    out[...] = source[...]


def leave(table, states):
    return pl.pallas_call(
        copy_kernel,
        grid_spec=pltpu.PrefetchScalarGridSpec(
            num_scalar_prefetch=1,
            grid=(HALF,),
            in_specs=[pl.BlockSpec(STATE, lambda q, sc: (sc[LEAVE + q], 0, 0, 0))],
            out_specs=pl.BlockSpec(STATE, lambda q, sc: (q, 0, 0, 0)),
        ),
        out_shape=jax.ShapeDtypeStruct((HALF, 8, 64, 128), BF16),
        compiler_params=LIMIT,
        cost_estimate=FREE,
        name="leave",
    )(table, states)


def pick_kernel(count, start, start_row, sc, *refs):
    sources, out, sems = refs[:count], refs[-2], refs[-1]
    slots = out.shape[0]
    for q in range(slots):
        for which in range(count):

            @pl.when(sc[start + q] == which)
            def _():
                row = sc[start_row + q]
                pltpu.make_async_copy(sources[which].at[row], out.at[q], sems.at[q]).start()

    for q in range(slots):
        pltpu.make_async_copy(sources[0].at[0], out.at[q], sems.at[q]).wait()


def pick(table, sources, start, start_row, slots, after):
    return pl.pallas_call(
        functools.partial(pick_kernel, len(sources), start, start_row),
        grid_spec=pltpu.PrefetchScalarGridSpec(
            num_scalar_prefetch=1,
            grid=(1,),
            in_specs=[ANYWHERE] * (len(sources) + 1),
            out_specs=pl.BlockSpec(memory_space=pltpu.VMEM),
            scratch_shapes=[pltpu.SemaphoreType.DMA((slots,))],
        ),
        out_shape=jax.ShapeDtypeStruct((slots, 8, 64, 128), BF16),
        compiler_params=LIMIT,
        cost_estimate=FREE,
        name="pick",
    )(table, *sources, after)


def local(
    ssm_input,
    gate_input,
    write_basis,
    read_basis,
    step_raw,
    step_bias,
    decay_rate,
    skip_gain,
    norm_gain,
    out_weight,
    ssm_states,
    anchor,
    tool_length,
):
    place = jnp.stack([lax.axis_index(n) for n in ("y", "zl", "c", "x", "zh")]).astype(jnp.int32)
    table = route(place, tool_length, anchor)
    buf = leave(table, ssm_states)
    along = [buf] + [shift(buf, "y", k) for k in (1, 2, 3)]

    shares = slices(table, out_weight, buf, 0, 2)
    got = [flip(shares[0], 1), flip(shares[1], 3)]

    b = write_basis.reshape(ROWS, 4 * NEW, 128)
    c = read_basis.reshape(ROWS, 4 * NEW, 128)
    gain = norm_gain.reshape(1, 512)
    ssm = functools.partial(
        run_ssm,
        table,
        x=ssm_input,
        gate=gate_input,
        b=b,
        c=c,
        dt=step_raw,
        scalars=(step_bias, decay_rate, skip_gain),
    )

    def spread_rows(gated, sums, after):
        a = normalise(gated, sums, gain, after)
        return a, [flip(a, 1), flip(a, 3)]

    def reduce_rest(base, moved, after, part=0):
        zs = combine(table, base, *moved, after, part)
        return [zs[0]] + [shift(zs[k], "zh", k) for k in (1, 2, 3)]

    gated1, sq1, states1 = ssm(start=0, sources=[ssm_states], alias=None, after=[shares[0]])
    sums1 = lax.psum(sq1, "zh")

    chosen = pick(table, along, BESIDE, BESIDE_ROW, 8, sums1)
    beside = shift(chosen, "c", 1)
    near_weights = join(*got, wait(chosen))
    a1, nears1 = spread_rows(gated1, [sums1], near_weights)
    picked = pick(table, [*along, beside], ACROSS, ACROSS_ROW, HALF, a1)
    across = shift(picked, "zl", 1)
    near_weights = hold(near_weights, picked)
    weights = [near_weights, shift(near_weights, "c", 1)]
    part0, part1, own = slices(table, out_weight, picked, 2, 5)
    sent1 = project(table, a1, nears1, [part0, part1], weights, picked)
    moved1 = [flip(sent1[0], 3), flip(sent1[1], 1)]
    base1 = base_project(table, a1, nears1, own, weights, sent1[0])

    gated2, sq2, new_states = ssm(
        start=HALF, sources=[ssm_states, *along, beside, across], alias=states1, after=[sent1[0]]
    )
    near_sums = trade(sq2, 1)
    z0, r1, r2, r3 = reduce_rest(base1, moved1, [sq2])
    half_sums = add(sq2, near_sums, z0)
    a2, nears2 = spread_rows(gated2, [half_sums, trade(half_sums, 3)], z0)
    gathered = gather_sum([z0, r1, r3], F32)
    sent2 = project(table, a2, nears2, [part0, part1], weights, gathered, 2)
    moved2 = [[flip(sent2[k], 3), flip(sent2[2 + k], 1)] for k in range(2)]
    base2 = base_project(table, a2, nears2, own, weights, sent2[0])
    z0, r1, late, r3 = reduce_rest(base2, moved2[0], [base2], 0)
    gathered2 = gather_sum([z0, r1, r3], F32)
    half_out = gather_sum([gathered, r2], BF16)
    done2 = reduce_rest(base2, moved2[1], [half_out, gathered2], 1)
    return finish(table, half_out, [gathered2, late, *done2]), new_states


def solution(mesh):
    fine = Mesh(mesh.devices.reshape(4, 2, 2, 4, 4), ("y", "zl", "c", "x", "zh"))
    dp, tp = ("y", "zl", "c"), ("x", "zh")
    placed = (
        P(dp, None, tp),
        P(dp, None, tp),
        P(dp, None, None, None),
        P(dp, None, None, None),
        P(dp, tp, None),
        P(tp),
        P(tp),
        P(tp),
        P(tp),
        P(tp, None),
        P(dp, tp, None, None),
        P(),
        P(dp),
    )
    return jax.shard_map(
        local,
        mesh=fine,
        in_specs=placed,
        out_specs=(P(dp, None, tp), P(dp, tp, None, None)),
        check_vma=False,
    )
```
